512 devices in a mesh: inst: 64 (over z, y), tp: 8 (over x, core).
Axes of the slice: x: 4, y: 4, z: 16, core: 2. Of those that a mesh axis runs over, the one named last changes fastest.
Arguments:
- queries: bfloat16 [512, 8192], P(('inst', 'tp')), may hold values from -6 to 6
- kv_pool: bfloat16 [2, 2048, 256, 1024], P(None, 'inst', None, 'tp'), may hold values from -6 to 6
- block_table: int32 [512, 4], P('inst'), may hold values from 0 to 2047, as said below
- lengths: int32 [512], P('inst'), may hold values from 1 to 1024, as said below
Outputs:
- attended: bfloat16 [512, 8192], P(('inst', 'tp'))
The draws below stay inside these ranges and needn't reach their ends.
Inputs may be any that keep to these rules, and one draw needn't show every extreme that they name: `block_table`: every number from 0 to 2047 appears exactly once; a slot number divided by 32 is the instance whose pool holds the block, its remainder the slot in that pool. `lengths`: some row has exactly 1024 tokens.
All inputs are finite; a program needn't handle non-finite values.
Results may differ from the reference program's by a relative error of at most 0.0041.
Values may be sent and summed in bfloat16 or wider, within the bound.
No kernel may reach another device: no remote copies, remote signals or barrier semaphores. Data moves between devices by JAX's collectives and lax.ppermute only.
A program may use at most 64 MiB of HBM per device.

```python
import math
import jax
import jax.numpy as jnp
from jax import lax

H = 64
KVH = 8
HD = 128
BLK = 256
MAXB = 4
ROWS = 512
GSLOTS = 2048
MAXLEN = 1024


def draw_queries(key, part):
    key = jax.random.fold_in(key, 11)
    key_one = jax.random.fold_in(key, 0)
    values = jnp.clip(jax.random.normal(key_one, (ROWS, H, HD), jnp.float32), -6.0, 6.0)
    return values.reshape(ROWS, H * HD).astype(jnp.bfloat16)


def draw_kv_pool(key, part):
    key = jax.random.fold_in(key, 23)
    key_one = jax.random.fold_in(key, 0)
    values = jnp.clip(jax.random.normal(key_one, (2, GSLOTS, BLK, KVH, HD), jnp.float32), -6.0, 6.0)
    return values.reshape(2, GSLOTS, BLK, KVH * HD).astype(jnp.bfloat16)


def draw_block_table(key, part):
    key = jax.random.fold_in(key, 37)
    order = jax.random.permutation(key, ROWS * MAXB)
    return order.reshape(ROWS, MAXB).astype(jnp.int32)


def draw_lengths(key, part):
    key = jax.random.fold_in(key, 41)
    key_one, key_two = jax.random.split(key)
    drawn = jax.random.randint(key_one, (ROWS,), 1, MAXLEN + 1)
    chosen = jax.random.randint(key_two, (), 0, ROWS)
    return jnp.where(jnp.arange(ROWS) == chosen, MAXLEN, drawn).astype(jnp.int32)


def setup_inputs(seed: int = 0) -> dict:
    keys = jax.random.split(jax.random.key(seed), 5)
    queries = draw_queries(jax.random.fold_in(keys[4], 71), 0)
    kv_pool = draw_kv_pool(jax.random.fold_in(keys[4], 71), 0)
    block_table = draw_block_table(jax.random.fold_in(keys[4], 71), 0)
    lengths = draw_lengths(jax.random.fold_in(keys[4], 71), 0)
    return dict(queries=queries, kv_pool=kv_pool, block_table=block_table, lengths=lengths)


def reference(queries, kv_pool, block_table, lengths):
    group_size = H // KVH
    score_scale = 1.0 / math.sqrt(HD)

    def one_row(items):
        query, slot_ids, length = items
        slot_keys = kv_pool[0][slot_ids].astype(jnp.float32).reshape(MAXB, BLK, KVH, HD)
        slot_values = kv_pool[1][slot_ids].astype(jnp.float32).reshape(MAXB, BLK, KVH, HD)
        heads = query.astype(jnp.float32).reshape(KVH, group_size, HD)
        scores = jnp.einsum('kgd,btkd->kgbt', heads, slot_keys) * score_scale
        position = jnp.arange(MAXB)[:, None] * BLK + jnp.arange(BLK)[None, :]
        valid = position < length
        scores = jnp.where(valid, scores, -1e+30)
        block_peak = lax.optimization_barrier(jnp.max(scores, axis=3))
        exponent = jnp.where(valid, jnp.exp(scores - block_peak[..., None]), 0.0)
        block_sum = lax.optimization_barrier(jnp.sum(exponent, axis=3))
        weights = exponent.astype(jnp.bfloat16).astype(jnp.float32)
        mixture = jnp.einsum('kgbt,btkd->kgbd', weights, slot_values)
        block_ok = jnp.arange(MAXB) * BLK < length
        partial_value = mixture / jnp.where(block_ok, block_sum, 1.0)[..., None]
        peak_ok = jnp.where(block_ok, block_peak, -1e+30)
        overall = lax.optimization_barrier(jnp.max(peak_ok, axis=2))
        factor = jnp.where(block_ok, jnp.exp(peak_ok - overall[..., None]) * block_sum, 0.0)
        numerator = lax.optimization_barrier(jnp.sum(factor[..., None] * partial_value, axis=2))
        denominator = lax.optimization_barrier(jnp.sum(factor, axis=2))
        result = numerator / denominator[..., None]
        return result.reshape(H * HD).astype(jnp.bfloat16)
    return lax.map(one_row, (queries, block_table, lengths))
```

```python
import functools
import math

import jax
import jax.numpy as jnp
from jax import lax
from jax.experimental import pallas as pl
from jax.experimental.pallas import tpu as pltpu
from jax.sharding import Mesh, PartitionSpec as P

HD = 128
NY = 4
TP = 8
GROUP = 8
MAXB = 4
BLK = 256
SLOTS = 32
ROWS = NY * TP
WIDE = GROUP * HD
LANES = WIDE + HD
NEG = -1e30
F32 = jnp.float32
BF16 = jnp.bfloat16


def dot(a, b, dims):
    return lax.dot_general(a, b, (dims, ((), ())), preferred_element_type=F32)


def split(x):
    hi = x.astype(BF16).astype(F32)
    mid = (x - hi).astype(BF16).astype(F32)
    return hi, mid, x - hi - mid


def lanes(shape):
    return lax.broadcasted_iota(jnp.int32, shape, len(shape) - 1)


def fan_kernel(me_ref, table_ref, len_ref, q_ref, out_ref):
    t = me_ref[0]
    lane = lanes((TP, GROUP, HD))
    extra = jnp.zeros((TP, GROUP, HD), F32)
    for b in range(MAXB):
        slot = table_ref[t, b]
        extra = jnp.where(lane == b, (slot // SLOTS).astype(F32), extra)
        extra = jnp.where(lane == MAXB + b, (slot % SLOTS).astype(F32), extra)
    length = len_ref[t]
    extra = jnp.where(lane == 8, (length // SLOTS).astype(F32), extra)
    extra = jnp.where(lane == 9, (length % SLOTS).astype(F32), extra)
    q = q_ref[...].astype(F32)
    heads = jnp.concatenate([q[:, h * HD : (h + 1) * HD] for h in range(TP * GROUP)], axis=0)
    both = jnp.concatenate([heads.reshape(TP, GROUP, HD), extra], axis=1).astype(BF16)
    for y in range(NY):
        out_ref[y * TP : (y + 1) * TP] = both


def pack_kernel(cap, me_ref, a_ref, out_ref, map_ref, scr):
    y = me_ref[1].astype(F32)
    targets = out_ref.shape[0]
    scr[...] = a_ref[...].reshape(ROWS * 16, HD).astype(F32)
    query = jnp.concatenate(
        [scr[pl.ds(g, ROWS, stride=16), :] for g in range(GROUP)], axis=1
    ).astype(BF16)
    extra = scr[pl.ds(GROUP, ROWS, stride=16), :]
    pool = jnp.concatenate([extra[:, b : b + 1] for b in range(MAXB)], axis=0)
    slot = jnp.concatenate([extra[:, MAXB + b : MAXB + b + 1] for b in range(MAXB)], axis=0)
    length = extra[:, 8:9] * SLOTS + extra[:, 9:10]
    filled = jnp.concatenate([length - b * BLK for b in range(MAXB)], axis=0)
    filled = jnp.clip(filled, 0.0, float(BLK))
    dest = jnp.floor(pool * (1.0 / NY))
    valid = (pool - dest * NY == y) & (filled > 0.0)
    entries = MAXB * ROWS
    lane = lanes((entries, HD)).astype(F32)
    member = jnp.where((lane == dest) & valid, 1.0, 0.0)
    earlier = jnp.where(
        lax.broadcasted_iota(jnp.int32, (entries, entries), 0) > lanes((entries, entries)), 1.0, 0.0
    ).astype(BF16)
    before = dot(earlier, member.astype(BF16), ((1,), (0,)))
    rank = jnp.sum(before * member, axis=1, keepdims=True)
    most = jnp.max(jnp.sum(member, axis=0, keepdims=True))
    target = jnp.where(valid & (rank < cap), dest * cap + rank, -1.0)
    place = jnp.where(lanes((entries, targets)).astype(F32) == target, 1.0, 0.0).astype(BF16)
    map_ref[...] = place
    lane = lanes((entries, HD))
    mine = jnp.where(lane == 0, slot + 1.0, jnp.where(lane == 1, filled, 0.0)).astype(BF16)
    four = jnp.concatenate([query] * MAXB, axis=0)
    out_ref[:, :WIDE] = dot(place, four, ((0,), (0,))).astype(BF16)
    extra = dot(place, mine, ((0,), (0,)))
    out_ref[:, WIDE:] = jnp.where(lanes((targets, HD)) == 2, most, extra).astype(BF16)


def attend_kernel(b_ref, kv_ref, out_ref, q_scr, f_scr, s_scr, p_scr, o_scr):
    targets = b_ref.shape[0]
    slot = b_ref[:, WIDE : WIDE + HD].astype(F32)[:, 0:1] - 1.0
    place = jnp.where(lanes((targets, SLOTS)).astype(F32) == slot, 1.0, 0.0).astype(BF16)
    got = dot(place, b_ref[...], ((0,), (0,)))
    for g in range(GROUP):
        rows = pl.ds(g, SLOTS, stride=GROUP)
        q_scr[rows, :] = got[:, g * HD : (g + 1) * HD]
        f_scr[rows, :] = jnp.broadcast_to(got[:, WIDE + 1 : WIDE + 2], (SLOTS, HD))
    for s in range(SLOTS):
        rows = slice(s * GROUP, (s + 1) * GROUP)
        s_scr[rows, :] = dot(q_scr[rows, :].astype(BF16), kv_ref[0, s], ((1,), (1,)))
    scores = s_scr[...] * (1.0 / math.sqrt(HD))
    mask = lanes((SLOTS * GROUP, BLK)).astype(F32) < f_scr[:, 0:1]
    scores = jnp.where(mask, scores, NEG)
    peak = jnp.max(scores, axis=1, keepdims=True)
    expo = jnp.where(mask, jnp.exp(scores - peak), 0.0)
    total = jnp.sum(expo, axis=1, keepdims=True)
    used = total > 0.0
    total = jnp.where(used, total, 1.0)
    p_scr[...] = expo
    for s in range(SLOTS):
        rows = slice(s * GROUP, (s + 1) * GROUP)
        o_scr[rows, :] = dot(p_scr[rows, :].astype(BF16), kv_ref[1, s], ((1,), (0,)))
    o_scr[...] = o_scr[...] / total
    level = jnp.where(used, peak + jnp.log(total), NEG)
    f_scr[...] = jnp.broadcast_to(level, (SLOTS * GROUP, HD))
    lane = lanes((SLOTS, HD))
    extra = jnp.zeros((SLOTS, HD), F32)
    parts = []
    for g in range(GROUP):
        rows = pl.ds(g, SLOTS, stride=GROUP)
        parts.append(o_scr[rows, :])
        for k, part in enumerate(split(f_scr[rows, :])):
            extra = jnp.where(lane == 3 * g + k, part, extra)
    back = jnp.concatenate(parts + [extra], axis=1).astype(BF16)
    out_ref[...] = dot(place, back, ((1,), (0,))).astype(BF16)


def gather_kernel(map_ref, c_ref, out_ref, scr):
    got, ok = [], []
    for b in range(MAXB):
        place = map_ref[b * ROWS : (b + 1) * ROWS, :]
        got.append(dot(place, c_ref[...], ((1,), (0,))))
        ok.append(jnp.sum(place.astype(F32), axis=1, keepdims=True) > 0.0)
    lane = lanes((ROWS, HD))
    for g in range(GROUP):
        level = []
        for b in range(MAXB):
            three = got[b][:, WIDE + 3 * g : WIDE + 3 * g + 3]
            level.append(jnp.where(ok[b], jnp.sum(three, axis=1, keepdims=True), NEG))
        top = functools.reduce(jnp.maximum, level)
        factor = [jnp.where(ok[b], jnp.exp(level[b] - top), 0.0) for b in range(MAXB)]
        total = functools.reduce(jnp.add, factor)
        any_ok = total > 0.0
        total = jnp.where(any_ok, total, 1.0)
        mixed = functools.reduce(
            jnp.add, [factor[b] * got[b][:, g * HD : (g + 1) * HD] for b in range(MAXB)]
        )
        scr[pl.ds(g, ROWS, stride=16), :] = mixed / total
        hi, mid, lo = split(jnp.where(any_ok, top + jnp.log(total), NEG))
        scr[pl.ds(GROUP + g, ROWS, stride=16), :] = jnp.where(
            lane == 0, hi, jnp.where(lane == 1, mid, jnp.where(lane == 2, lo, 0.0))
        )
    out_ref[...] = scr[...].reshape(ROWS, 16, HD).astype(BF16)


def finish_kernel(d_ref, out_ref):
    parts, level = [], []
    for y in range(NY):
        x = d_ref[y * TP : (y + 1) * TP].astype(F32)
        parts.append(x[:, :GROUP, :])
        level.append(jnp.sum(x[:, GROUP:, :], axis=2, keepdims=True))
    top = functools.reduce(jnp.maximum, level)
    factor = [jnp.exp(one - top) for one in level]
    total = functools.reduce(jnp.add, factor)
    mixed = functools.reduce(jnp.add, [f * p for f, p in zip(factor, parts)])
    result = (mixed / total).reshape(TP * GROUP, HD)
    out_ref[...] = jnp.concatenate(
        [result[h : h + 1, :] for h in range(TP * GROUP)], axis=1
    ).astype(BF16)


SMEM = pl.BlockSpec(memory_space=pltpu.SMEM)
VMEM = pl.BlockSpec(memory_space=pltpu.VMEM)


def call(kernel, out, ins, scratch=(), limit=32 << 20):
    return pl.pallas_call(
        kernel,
        out_shape=out,
        in_specs=ins,
        out_specs=jax.tree.map(lambda _: VMEM, out),
        scratch_shapes=scratch,
        compiler_params=pltpu.CompilerParams(vmem_limit_bytes=limit),
    )


def shape(dims, dtype=BF16):
    return jax.ShapeDtypeStruct(dims, dtype)


def per_device(cap, queries, kv_pool, block_table, lengths):
    nz = lax.axis_size("z")
    me = jnp.stack([lax.axis_index(("x", "c")), lax.axis_index("y")]).astype(jnp.int32)

    def over_plane(x):
        return lax.all_to_all(x, ("y", "x", "c"), 0, 0, tiled=True)

    def along_z(x, c):
        x = lax.all_to_all(x.reshape(nz, c, LANES), "z", 0, 0, tiled=True)
        return x.reshape(nz * c, LANES)

    def pack(rows, c):
        out, place = call(
            functools.partial(pack_kernel, c),
            (shape((nz * c, LANES)), shape((MAXB * ROWS, nz * c))),
            [SMEM, VMEM],
            [pltpu.VMEM((ROWS * 16, HD), F32)],
        )(me, rows)
        return along_z(out, c), place

    def attend(got, place, c):
        back = call(
            attend_kernel,
            shape((nz * c, LANES)),
            [VMEM, VMEM],
            [
                pltpu.VMEM((SLOTS * GROUP, HD), F32),
                pltpu.VMEM((SLOTS * GROUP, HD), F32),
                pltpu.VMEM((SLOTS * GROUP, BLK), F32),
                pltpu.VMEM((SLOTS * GROUP, BLK), F32),
                pltpu.VMEM((SLOTS * GROUP, HD), F32),
            ],
        )(got, kv_pool)
        return call(
            gather_kernel,
            shape((ROWS, 16, HD)),
            [VMEM, VMEM],
            [pltpu.VMEM((ROWS * 16, HD), F32)],
        )(place, along_z(back, c))

    fanned = call(fan_kernel, shape((ROWS, 16, HD)), [SMEM, SMEM, SMEM, VMEM])(
        me, block_table, lengths, queries
    )
    rows = over_plane(fanned)
    got, place = pack(rows, cap)
    most = jnp.max(got.reshape(nz, cap, LANES)[:, 0, WIDE + 2])
    mixed = lax.cond(
        most > cap,
        lambda: attend(*pack(rows, SLOTS), SLOTS),
        lambda: attend(got, place, cap),
    )
    return call(finish_kernel, shape((1, TP * WIDE)), [VMEM])(over_plane(mixed))


def solution(mesh):
    fine = Mesh(mesh.devices.reshape(-1, NY, TP // 2, 2), ("z", "y", "x", "c"))
    own = ("z", "y", "x", "c")
    return jax.shard_map(
        functools.partial(per_device, 8),
        mesh=fine,
        in_specs=(
            P(own, None),
            P(None, ("z", "y"), None, ("x", "c")),
            P(("z", "y"), None),
            P(("z", "y")),
        ),
        out_specs=P(own, None),
        check_vma=False,
    )
```

```python
import functools
import math

import jax
import jax.numpy as jnp
from jax import lax
from jax.experimental import pallas as pl
from jax.experimental.pallas import tpu as pltpu
from jax.sharding import Mesh, PartitionSpec as P

HD = 128
NY = 4
TP = 8
GROUP = 8
MAXB = 4
BLK = 256
SLOTS = 32
ROWS = NY * TP
WIDE = GROUP * HD
NEG = -1e30
F32 = jnp.float32
BF16 = jnp.bfloat16


def dot(a, b, dims):
    return lax.dot_general(a, b, (dims, ((), ())), preferred_element_type=F32)


def split(x):
    hi = x.astype(BF16).astype(F32)
    mid = (x - hi).astype(BF16).astype(F32)
    return hi, mid, x - hi - mid


def lanes(shape):
    return lax.broadcasted_iota(jnp.int32, shape, len(shape) - 1)


def fan_kernel(q_hbm, table_hbm, len_hbm, out_ref, q_ref, table_ref, len_ref, sems):
    copies = [
        pltpu.make_async_copy(q_hbm, q_ref, sems.at[0]),
        pltpu.make_async_copy(table_hbm, table_ref, sems.at[1]),
        pltpu.make_async_copy(len_hbm, len_ref, sems.at[2]),
    ]
    for copy in copies:
        copy.start()
    for copy in copies:
        copy.wait()
    t = lax.axis_index("x") * 2 + lax.axis_index("c")
    lane = lanes((TP, GROUP, HD))
    extra = jnp.zeros((TP, GROUP, HD), F32)
    for b in range(MAXB):
        slot = table_ref[b, t]
        extra = jnp.where(lane == b, (slot // SLOTS).astype(F32), extra)
        extra = jnp.where(lane == MAXB + b, (slot % SLOTS).astype(F32), extra)
    length = len_ref[t]
    extra = jnp.where(lane == 8, (length // SLOTS).astype(F32), extra)
    extra = jnp.where(lane == 9, (length % SLOTS).astype(F32), extra)
    q = q_ref[...].astype(F32)
    heads = jnp.concatenate([q[:, h * HD : (h + 1) * HD] for h in range(TP * GROUP)], axis=0)
    both = jnp.concatenate([heads.reshape(TP, GROUP, HD), extra], axis=1).astype(BF16)
    for y in range(NY):
        out_ref[y * TP : (y + 1) * TP] = both


def pack_kernel(cap, skip, a_ref, out_ref, map_ref, scr):
    y = lax.axis_index("y").astype(F32)
    targets = out_ref.shape[0]
    tall = cap + 1
    scr[...] = a_ref[...].reshape(ROWS * 16, HD).astype(F32)
    query = jnp.concatenate(
        [scr[pl.ds(g, ROWS, stride=16), :] for g in range(GROUP)], axis=1
    ).astype(BF16)
    extra = scr[pl.ds(GROUP, ROWS, stride=16), :]
    pool = jnp.concatenate([extra[:, b : b + 1] for b in range(MAXB)], axis=0)
    slot = jnp.concatenate([extra[:, MAXB + b : MAXB + b + 1] for b in range(MAXB)], axis=0)
    length = extra[:, 8:9] * SLOTS + extra[:, 9:10]
    filled = jnp.concatenate([length - b * BLK for b in range(MAXB)], axis=0)
    filled = jnp.clip(filled, 0.0, float(BLK))
    dest = jnp.floor(pool * (1.0 / NY))
    valid = (pool - dest * NY == y) & (filled > 0.0)
    entries = MAXB * ROWS
    lane = lanes((entries, HD))
    member = jnp.where((lane.astype(F32) == dest) & valid, 1.0, 0.0)
    earlier = jnp.where(
        lax.broadcasted_iota(jnp.int32, (entries, entries), 0) > lanes((entries, entries)), 1.0, 0.0
    ).astype(BF16)
    before = dot(earlier, member.astype(BF16), ((1,), (0,)))
    rank = jnp.sum(before * member, axis=1, keepdims=True)
    most = jnp.max(jnp.sum(member, axis=0, keepdims=True))
    rank = rank - skip
    fits = valid & (rank >= 0.0) & (rank < cap)
    column = lanes((entries, targets)).astype(F32)
    place = jnp.where(column == jnp.where(fits, dest * tall + rank, -1.0), 1.0, 0.0).astype(BF16)
    last = jnp.where(column == jnp.where(fits, dest * tall + cap, -1.0), 1.0, 0.0).astype(BF16)
    map_ref[...] = place
    mine = jnp.where(lane % 2 == 0, slot + 1.0, filled)
    mine = jnp.where((lane // 2).astype(F32) == rank, mine, 0.0).astype(BF16)
    four = jnp.concatenate([query] * MAXB, axis=0)
    out_ref[...] = dot(place, four, ((0,), (0,))).astype(BF16)
    numbers = dot(last, mine, ((0,), (0,)))
    numbers = jnp.where(lanes((targets, HD)) == 2 * cap, most, numbers)
    final = lax.broadcasted_iota(jnp.int32, (targets, HD), 0) % tall == cap
    head = out_ref[:, :HD].astype(F32)
    out_ref[:, :HD] = jnp.where(final, numbers, head).astype(BF16)


def own_lanes(x, tall, width):
    groups = x.shape[0] // tall
    x = x.astype(F32).reshape(groups, tall, HD)
    last = jnp.broadcast_to(x[:, tall - 1 : tall, :], (groups, tall, HD))
    row = lax.broadcasted_iota(jnp.int32, (groups, tall, HD), 1)
    mine = (lanes((groups, tall, HD)) // width == row) & (row < tall - 1)
    return jnp.where(mine, last, 0.0).reshape(groups * tall, HD)


def attend_kernel(cap, b_ref, kv_ref, out_ref, most_ref, q_scr, f_scr, s_scr, p_scr, o_scr):
    targets = b_ref.shape[0]
    tall = cap + 1
    numbers = b_ref[:, :HD]
    lane = lanes((targets, HD))
    row = lax.broadcasted_iota(jnp.int32, (targets, HD), 0)
    most = jnp.max(
        jnp.where((row % tall == cap) & (lane == 2 * cap), numbers.astype(F32), 0.0)
    )
    most_ref[0] = jnp.where(most > 2 * cap, 2, jnp.where(most > cap, 1, 0))
    own = own_lanes(numbers, tall, 2)
    slot = jnp.sum(jnp.where(lane % 2 == 0, own, 0.0), axis=1, keepdims=True) - 1.0
    filled = jnp.sum(jnp.where(lane % 2 == 1, own, 0.0), axis=1, keepdims=True)
    place = jnp.where(lanes((targets, SLOTS)).astype(F32) == slot, 1.0, 0.0).astype(BF16)
    got = dot(place, b_ref[...], ((0,), (0,)))
    filled = jnp.broadcast_to(filled, (targets, HD)).astype(BF16)
    filled = dot(place, filled, ((0,), (0,)))
    for g in range(GROUP):
        rows = pl.ds(g, SLOTS, stride=GROUP)
        q_scr[rows, :] = got[:, g * HD : (g + 1) * HD]
        f_scr[rows, :] = filled
    for s in range(SLOTS):
        rows = slice(s * GROUP, (s + 1) * GROUP)
        s_scr[rows, :] = dot(q_scr[rows, :].astype(BF16), kv_ref[0, s], ((1,), (1,)))
    scores = s_scr[...] * (1.0 / math.sqrt(HD))
    mask = lanes((SLOTS * GROUP, BLK)).astype(F32) < f_scr[:, 0:1]
    scores = jnp.where(mask, scores, NEG)
    peak = jnp.max(scores, axis=1, keepdims=True)
    expo = jnp.where(mask, jnp.exp(scores - peak), 0.0)
    total = jnp.sum(expo, axis=1, keepdims=True)
    used = total > 0.0
    total = jnp.where(used, total, 1.0)
    p_scr[...] = expo
    for s in range(SLOTS):
        rows = slice(s * GROUP, (s + 1) * GROUP)
        o_scr[rows, :] = dot(p_scr[rows, :].astype(BF16), kv_ref[1, s], ((1,), (0,)))
    o_scr[...] = o_scr[...] / total
    level = jnp.where(used, peak + jnp.log(total), NEG)
    f_scr[...] = jnp.broadcast_to(level, (SLOTS * GROUP, HD))
    lane = lanes((SLOTS, HD)) % 16
    coarse = jnp.zeros((SLOTS, HD), F32)
    fine = jnp.zeros((SLOTS, HD), F32)
    parts = []
    for g in range(GROUP):
        rows = pl.ds(g, SLOTS, stride=GROUP)
        parts.append(o_scr[rows, :])
        hi, mid, lo = split(f_scr[rows, :])
        coarse = jnp.where(lane == 2 * g, hi, jnp.where(lane == 2 * g + 1, mid, coarse))
        fine = jnp.where(lane == 2 * g, lo, fine)
    back = jnp.concatenate(parts, axis=1).astype(BF16)
    out_ref[...] = dot(place, back, ((1,), (0,))).astype(BF16)
    final = row % tall == cap
    lane = lanes((targets, HD))
    for k, part in enumerate((coarse, fine)):
        each = dot(place, part.astype(BF16), ((1,), (0,)))
        each = jnp.where(lane // 16 == row % tall, each, 0.0).reshape(targets // tall, tall, HD)
        both = jnp.broadcast_to(jnp.sum(each, axis=1, keepdims=True), each.shape)
        spot = slice(k * HD, (k + 1) * HD)
        head = out_ref[:, spot].astype(F32)
        out_ref[:, spot] = jnp.where(final, both.reshape(targets, HD), head).astype(BF16)


def gather_kernel(cap, map_ref, c_ref, out_ref, scr):
    tall = cap + 1
    coarse = own_lanes(c_ref[:, :HD], tall, 16).astype(BF16)
    fine = own_lanes(c_ref[:, HD : 2 * HD], tall, 16).astype(BF16)
    pick = lax.broadcasted_iota(jnp.int32, (HD, HD), 0) % 16 // 2 == lanes((HD, HD))
    pick = jnp.where(pick, 1.0, 0.0).astype(BF16)
    got, ok, levels = [], [], []
    for b in range(MAXB):
        place = map_ref[b * ROWS : (b + 1) * ROWS, :]
        got.append(dot(place, c_ref[...], ((1,), (0,))))
        ok.append(jnp.sum(place.astype(F32), axis=1, keepdims=True) > 0.0)
        level = 0.0
        for part in (coarse, fine):
            part = dot(place, part, ((1,), (0,))).astype(BF16)
            level = level + dot(part, pick, ((1,), (0,)))
        levels.append(level)
    lane = lanes((ROWS, HD))
    top = functools.reduce(
        jnp.maximum, [jnp.where(o, level, NEG) for o, level in zip(ok, levels)]
    )
    factor = [jnp.where(o, jnp.exp(level - top), 0.0) for o, level in zip(ok, levels)]
    total = functools.reduce(jnp.add, factor)
    any_ok = total > 0.0
    total = jnp.where(any_ok, total, 1.0)
    three = split(jnp.where(any_ok, top + jnp.log(total), NEG))
    factor = [f / total for f in factor]
    for g in range(GROUP):
        mixed = functools.reduce(
            jnp.add,
            [factor[b][:, g : g + 1] * got[b][:, g * HD : (g + 1) * HD] for b in range(MAXB)],
        )
        scr[pl.ds(g, ROWS, stride=16), :] = mixed
        hi, mid, lo = [part[:, g : g + 1] for part in three]
        scr[pl.ds(GROUP + g, ROWS, stride=16), :] = jnp.where(
            lane == 0, hi, jnp.where(lane == 1, mid, jnp.where(lane == 2, lo, 0.0))
        )
    out_ref[...] = scr[...].reshape(ROWS, 16, HD).astype(BF16)


def finish_kernel(d_ref, out_ref):
    parts, level = [], []
    for y in range(NY):
        x = d_ref[y * TP : (y + 1) * TP].astype(F32)
        parts.append(x[:, :GROUP, :])
        level.append(jnp.sum(x[:, GROUP:, :], axis=2, keepdims=True))
    top = functools.reduce(jnp.maximum, level)
    factor = [jnp.exp(one - top) for one in level]
    total = functools.reduce(jnp.add, factor)
    mixed = functools.reduce(jnp.add, [f * p for f, p in zip(factor, parts)])
    result = (mixed / total).reshape(TP * GROUP, HD)
    out_ref[...] = jnp.concatenate(
        [result[h : h + 1, :] for h in range(TP * GROUP)], axis=1
    ).astype(BF16)


SMEM = pl.BlockSpec(memory_space=pltpu.SMEM)
VMEM = pl.BlockSpec(memory_space=pltpu.VMEM)
HBM = pl.BlockSpec(memory_space=pltpu.HBM)


def call(kernel, out, ins, scratch=(), outs=VMEM, limit=24 << 20):
    return pl.pallas_call(
        kernel,
        out_shape=out,
        in_specs=ins,
        out_specs=outs,
        scratch_shapes=scratch,
        compiler_params=pltpu.CompilerParams(vmem_limit_bytes=limit),
    )


def shape(*dims):
    return jax.ShapeDtypeStruct(dims, BF16)


def per_device(cap, queries, kv_pool, block_table, lengths):
    nz = lax.axis_size("z")
    targets = nz * (cap + 1)

    def over_plane(x):
        return lax.all_to_all(x, ("y", "x", "c"), 0, 0, tiled=True)

    def along_z(x):
        x = lax.all_to_all(x.reshape(nz, -1, WIDE), "z", 0, 0, tiled=True)
        return x.reshape(-1, WIDE)

    def pack(rows, skip):
        return call(
            functools.partial(pack_kernel, cap, skip),
            (shape(targets, WIDE), shape(MAXB * ROWS, targets)),
            [VMEM],
            [pltpu.VMEM((ROWS * 16, HD), F32)],
            (VMEM, VMEM),
        )(rows)

    def attend(got, kv):
        return call(
            functools.partial(attend_kernel, cap),
            (shape(targets, WIDE), jax.ShapeDtypeStruct((1,), jnp.int32)),
            [VMEM, VMEM],
            [
                pltpu.VMEM((SLOTS * GROUP, HD), F32),
                pltpu.VMEM((SLOTS * GROUP, HD), F32),
                pltpu.VMEM((SLOTS * GROUP, BLK), F32),
                pltpu.VMEM((SLOTS * GROUP, BLK), F32),
                pltpu.VMEM((SLOTS * GROUP, HD), F32),
            ],
            (VMEM, SMEM),
        )(got, kv)

    def gather(places, backs):
        backs = [along_z(back) for back in backs]
        return call(
            functools.partial(gather_kernel, cap),
            shape(ROWS, 16, HD),
            [VMEM, VMEM],
            [pltpu.VMEM((ROWS * 16, HD), F32)],
        )(jnp.concatenate(places, axis=1), jnp.concatenate(backs, axis=0))

    def rounds(count):
        places, backs = [place], [back]
        for k in range(1, count):
            out, more = pack(rows, k * cap)
            places.append(more)
            backs.append(attend(along_z(out), kv_pool)[0])
        return gather(places, backs)

    fanned = call(
        fan_kernel,
        shape(ROWS, 16, HD),
        [HBM, HBM, HBM],
        [
            pltpu.VMEM((1, TP * WIDE), BF16),
            pltpu.SMEM((MAXB, TP), jnp.int32),
            pltpu.SMEM((TP,), jnp.int32),
            pltpu.SemaphoreType.DMA((3,)),
        ],
    )(queries, block_table.T, lengths)
    rows = over_plane(fanned)
    out, place = pack(rows, 0)
    got = along_z(out)
    got, place, rows, kv_pool = lax.optimization_barrier((got, place, rows, kv_pool))
    back, over = attend(got, kv_pool)
    mixed = lax.switch(
        over[0], [lambda: rounds(1), lambda: rounds(2), lambda: rounds(-(-SLOTS // cap))]
    )
    return call(finish_kernel, shape(1, TP * WIDE), [VMEM])(over_plane(mixed))


def solution(mesh):
    fine = Mesh(mesh.devices.reshape(-1, NY, TP // 2, 2), ("z", "y", "x", "c"))
    own = ("z", "y", "x", "c")
    return jax.shard_map(
        functools.partial(per_device, 7),
        mesh=fine,
        in_specs=(
            P(own, None),
            P(None, ("z", "y"), None, ("x", "c")),
            P(("z", "y"), None),
            P(("z", "y")),
        ),
        out_specs=P(own, None),
        check_vma=False,
    )
```

```python
import functools
import math

import jax
import jax.numpy as jnp
from jax import lax
from jax.experimental import pallas as pl
from jax.experimental.pallas import tpu as pltpu
from jax.sharding import Mesh, PartitionSpec as P

HD = 128
NY = 4
TP = 8
GROUP = 8
MAXB = 4
BLK = 256
SLOTS = 32
ROWS = NY * TP
WIDE = GROUP * HD
NEG = -1e30
F32 = jnp.float32
BF16 = jnp.bfloat16


def dot(a, b, dims):
    return lax.dot_general(a, b, (dims, ((), ())), preferred_element_type=F32)


def split(x):
    hi = x.astype(BF16).astype(F32)
    mid = (x - hi).astype(BF16).astype(F32)
    return hi, mid, x - hi - mid


def lanes(shape):
    return lax.broadcasted_iota(jnp.int32, shape, len(shape) - 1)


def fan_kernel(q_hbm, table_hbm, len_hbm, out_ref, q_ref, table_ref, len_ref, sems):
    copies = [
        pltpu.make_async_copy(q_hbm, q_ref, sems.at[0]),
        pltpu.make_async_copy(table_hbm, table_ref, sems.at[1]),
        pltpu.make_async_copy(len_hbm, len_ref, sems.at[2]),
    ]
    for copy in copies:
        copy.start()
    for copy in copies:
        copy.wait()
    t = lax.axis_index("x") * 2 + lax.axis_index("c")
    lane = lanes((TP, GROUP, HD))
    extra = jnp.zeros((TP, GROUP, HD), F32)
    for b in range(MAXB):
        slot = table_ref[b, t]
        extra = jnp.where(lane == b, (slot // SLOTS).astype(F32), extra)
        extra = jnp.where(lane == MAXB + b, (slot % SLOTS).astype(F32), extra)
    length = len_ref[t]
    extra = jnp.where(lane == 8, (length // SLOTS).astype(F32), extra)
    extra = jnp.where(lane == 9, (length % SLOTS).astype(F32), extra)
    q = q_ref[...].astype(F32)
    heads = jnp.concatenate([q[:, h * HD : (h + 1) * HD] for h in range(TP * GROUP)], axis=0)
    both = jnp.concatenate([heads.reshape(TP, GROUP, HD), extra], axis=1).astype(BF16)
    for y in range(NY):
        out_ref[y * TP : (y + 1) * TP] = both


def pack_kernel(cap, skip, a_ref, kv_hbm, out_ref, map_ref, scr):
    y = lax.axis_index("y").astype(F32)
    targets = out_ref.shape[0]
    tall = cap + 1
    scr[...] = a_ref[...].reshape(ROWS * 16, HD).astype(F32)
    query = jnp.concatenate(
        [scr[pl.ds(g, ROWS, stride=16), :] for g in range(GROUP)], axis=1
    ).astype(BF16)
    extra = scr[pl.ds(GROUP, ROWS, stride=16), :]
    pool = jnp.concatenate([extra[:, b : b + 1] for b in range(MAXB)], axis=0)
    slot = jnp.concatenate([extra[:, MAXB + b : MAXB + b + 1] for b in range(MAXB)], axis=0)
    length = extra[:, 8:9] * SLOTS + extra[:, 9:10]
    filled = jnp.concatenate([length - b * BLK for b in range(MAXB)], axis=0)
    filled = jnp.clip(filled, 0.0, float(BLK))
    dest = jnp.floor(pool * (1.0 / NY))
    valid = (pool - dest * NY == y) & (filled > 0.0)
    entries = MAXB * ROWS
    lane = lanes((entries, HD))
    member = jnp.where((lane.astype(F32) == dest) & valid, 1.0, 0.0)
    earlier = jnp.where(
        lax.broadcasted_iota(jnp.int32, (entries, entries), 0) > lanes((entries, entries)), 1.0, 0.0
    ).astype(BF16)
    before = dot(earlier, member.astype(BF16), ((1,), (0,)))
    rank = jnp.sum(before * member, axis=1, keepdims=True)
    most = jnp.max(jnp.sum(member, axis=0, keepdims=True))
    rank = rank - skip
    fits = valid & (rank >= 0.0) & (rank < cap)
    column = lanes((entries, targets)).astype(F32)
    place = jnp.where(column == jnp.where(fits, dest * tall + rank, -1.0), 1.0, 0.0).astype(BF16)
    last = jnp.where(column == jnp.where(fits, dest * tall + cap, -1.0), 1.0, 0.0).astype(BF16)
    map_ref[...] = place
    mine = jnp.where(lane % 2 == 0, slot + 1.0, filled)
    mine = jnp.where((lane // 2).astype(F32) == rank, mine, 0.0).astype(BF16)
    four = jnp.concatenate([query] * MAXB, axis=0)
    out_ref[...] = dot(place, four, ((0,), (0,))).astype(BF16)
    numbers = dot(last, mine, ((0,), (0,)))
    numbers = jnp.where(lanes((targets, HD)) == 2 * cap, most, numbers)
    final = lax.broadcasted_iota(jnp.int32, (targets, HD), 0) % tall == cap
    head = out_ref[:, :HD].astype(F32)
    out_ref[:, :HD] = jnp.where(final, numbers, head).astype(BF16)


def own_lanes(x, tall, width):
    groups = x.shape[0] // tall
    x = x.astype(F32).reshape(groups, tall, HD)
    last = jnp.broadcast_to(x[:, tall - 1 : tall, :], (groups, tall, HD))
    row = lax.broadcasted_iota(jnp.int32, (groups, tall, HD), 1)
    mine = (lanes((groups, tall, HD)) // width == row) & (row < tall - 1)
    return jnp.where(mine, last, 0.0).reshape(groups * tall, HD)


def attend_kernel(cap, b_ref, kv_ref, out_ref, most_ref, q_scr, f_scr, s_scr, p_scr, o_scr):
    targets = b_ref.shape[0]
    tall = cap + 1
    numbers = b_ref[:, :HD]
    lane = lanes((targets, HD))
    row = lax.broadcasted_iota(jnp.int32, (targets, HD), 0)
    most = jnp.max(
        jnp.where((row % tall == cap) & (lane == 2 * cap), numbers.astype(F32), 0.0)
    )
    most_ref[0] = jnp.where(most > 2 * cap, 2, jnp.where(most > cap, 1, 0))
    own = own_lanes(numbers, tall, 2)
    slot = jnp.sum(jnp.where(lane % 2 == 0, own, 0.0), axis=1, keepdims=True) - 1.0
    filled = jnp.sum(jnp.where(lane % 2 == 1, own, 0.0), axis=1, keepdims=True)
    place = jnp.where(lanes((targets, SLOTS)).astype(F32) == slot, 1.0, 0.0).astype(BF16)
    got = dot(place, b_ref[...], ((0,), (0,)))
    filled = jnp.broadcast_to(filled, (targets, HD)).astype(BF16)
    filled = dot(place, filled, ((0,), (0,)))
    for g in range(GROUP):
        rows = pl.ds(g, SLOTS, stride=GROUP)
        q_scr[rows, :] = got[:, g * HD : (g + 1) * HD]
        f_scr[rows, :] = filled
    for s in range(SLOTS):
        rows = slice(s * GROUP, (s + 1) * GROUP)
        s_scr[rows, :] = dot(q_scr[rows, :].astype(BF16), kv_ref[0, s], ((1,), (1,)))
    scores = s_scr[...] * (1.0 / math.sqrt(HD))
    mask = lanes((SLOTS * GROUP, BLK)).astype(F32) < f_scr[:, 0:1]
    scores = jnp.where(mask, scores, NEG)
    peak = jnp.max(scores, axis=1, keepdims=True)
    expo = jnp.where(mask, jnp.exp(scores - peak), 0.0)
    total = jnp.sum(expo, axis=1, keepdims=True)
    used = total > 0.0
    total = jnp.where(used, total, 1.0)
    p_scr[...] = expo
    for s in range(SLOTS):
        rows = slice(s * GROUP, (s + 1) * GROUP)
        o_scr[rows, :] = dot(p_scr[rows, :].astype(BF16), kv_ref[1, s], ((1,), (0,)))
    o_scr[...] = o_scr[...] / total
    level = jnp.where(used, peak + jnp.log(total), NEG)
    f_scr[...] = jnp.broadcast_to(level, (SLOTS * GROUP, HD))
    lane = lanes((SLOTS, HD)) % 16
    coarse = jnp.zeros((SLOTS, HD), F32)
    fine = jnp.zeros((SLOTS, HD), F32)
    parts = []
    for g in range(GROUP):
        rows = pl.ds(g, SLOTS, stride=GROUP)
        parts.append(o_scr[rows, :])
        hi, mid, lo = split(f_scr[rows, :])
        coarse = jnp.where(lane == 2 * g, hi, jnp.where(lane == 2 * g + 1, mid, coarse))
        fine = jnp.where(lane == 2 * g, lo, fine)
    back = jnp.concatenate(parts, axis=1).astype(BF16)
    out_ref[...] = dot(place, back, ((1,), (0,))).astype(BF16)
    final = row % tall == cap
    lane = lanes((targets, HD))
    for k, part in enumerate((coarse, fine)):
        each = dot(place, part.astype(BF16), ((1,), (0,)))
        each = jnp.where(lane // 16 == row % tall, each, 0.0).reshape(targets // tall, tall, HD)
        both = jnp.broadcast_to(jnp.sum(each, axis=1, keepdims=True), each.shape)
        spot = slice(k * HD, (k + 1) * HD)
        head = out_ref[:, spot].astype(F32)
        out_ref[:, spot] = jnp.where(final, both.reshape(targets, HD), head).astype(BF16)


def gather_kernel(cap, map_ref, c_ref, out_ref, scr):
    tall = cap + 1
    coarse = own_lanes(c_ref[:, :HD], tall, 16).astype(BF16)
    fine = own_lanes(c_ref[:, HD : 2 * HD], tall, 16).astype(BF16)
    pick = lax.broadcasted_iota(jnp.int32, (HD, HD), 0) % 16 // 2 == lanes((HD, HD))
    pick = jnp.where(pick, 1.0, 0.0).astype(BF16)
    got, ok, levels = [], [], []
    for b in range(MAXB):
        place = map_ref[b * ROWS : (b + 1) * ROWS, :]
        got.append(dot(place, c_ref[...], ((1,), (0,))))
        ok.append(jnp.sum(place.astype(F32), axis=1, keepdims=True) > 0.0)
        level = 0.0
        for part in (coarse, fine):
            part = dot(place, part, ((1,), (0,))).astype(BF16)
            level = level + dot(part, pick, ((1,), (0,)))
        levels.append(level)
    lane = lanes((ROWS, HD))
    top = functools.reduce(
        jnp.maximum, [jnp.where(o, level, NEG) for o, level in zip(ok, levels)]
    )
    factor = [jnp.where(o, jnp.exp(level - top), 0.0) for o, level in zip(ok, levels)]
    total = functools.reduce(jnp.add, factor)
    any_ok = total > 0.0
    total = jnp.where(any_ok, total, 1.0)
    three = split(jnp.where(any_ok, top + jnp.log(total), NEG))
    factor = [f / total for f in factor]
    for g in range(GROUP):
        mixed = functools.reduce(
            jnp.add,
            [factor[b][:, g : g + 1] * got[b][:, g * HD : (g + 1) * HD] for b in range(MAXB)],
        )
        scr[pl.ds(g, ROWS, stride=16), :] = mixed
        hi, mid, lo = [part[:, g : g + 1] for part in three]
        scr[pl.ds(GROUP + g, ROWS, stride=16), :] = jnp.where(
            lane == 0, hi, jnp.where(lane == 1, mid, jnp.where(lane == 2, lo, 0.0))
        )
    out_ref[...] = scr[...].reshape(ROWS, 16, HD).astype(BF16)


def finish_kernel(d_ref, out_ref):
    parts, level = [], []
    for y in range(NY):
        x = d_ref[y * TP : (y + 1) * TP].astype(F32)
        parts.append(x[:, :GROUP, :])
        level.append(jnp.sum(x[:, GROUP:, :], axis=2, keepdims=True))
    top = functools.reduce(jnp.maximum, level)
    factor = [jnp.exp(one - top) for one in level]
    total = functools.reduce(jnp.add, factor)
    mixed = functools.reduce(jnp.add, [f * p for f, p in zip(factor, parts)])
    result = (mixed / total).reshape(TP * GROUP, HD)
    out_ref[...] = jnp.concatenate(
        [result[h : h + 1, :] for h in range(TP * GROUP)], axis=1
    ).astype(BF16)


SMEM = pl.BlockSpec(memory_space=pltpu.SMEM)
VMEM = pl.BlockSpec(memory_space=pltpu.VMEM)
HBM = pl.BlockSpec(memory_space=pltpu.HBM)


def call(kernel, out, ins, scratch=(), outs=VMEM, limit=24 << 20):
    return pl.pallas_call(
        kernel,
        out_shape=out,
        in_specs=ins,
        out_specs=outs,
        scratch_shapes=scratch,
        compiler_params=pltpu.CompilerParams(vmem_limit_bytes=limit),
    )


def shape(*dims):
    return jax.ShapeDtypeStruct(dims, BF16)


def per_device(cap, queries, kv_pool, block_table, lengths):
    nz = lax.axis_size("z")
    targets = nz * (cap + 1)

    def over_plane(x):
        return lax.all_to_all(x, ("y", "x", "c"), 0, 0, tiled=True)

    def along_z(x):
        x = lax.all_to_all(x.reshape(nz, -1, WIDE), "z", 0, 0, tiled=True)
        return x.reshape(-1, WIDE)

    def pack(rows, skip):
        return call(
            functools.partial(pack_kernel, cap, skip),
            (shape(targets, WIDE), shape(MAXB * ROWS, targets)),
            [VMEM, HBM],
            [pltpu.VMEM((ROWS * 16, HD), F32)],
            (VMEM, VMEM),
        )(rows, kv_pool)

    def attend(got):
        return call(
            functools.partial(attend_kernel, cap),
            (shape(targets, WIDE), jax.ShapeDtypeStruct((1,), jnp.int32)),
            [VMEM, VMEM],
            [
                pltpu.VMEM((SLOTS * GROUP, HD), F32),
                pltpu.VMEM((SLOTS * GROUP, HD), F32),
                pltpu.VMEM((SLOTS * GROUP, BLK), F32),
                pltpu.VMEM((SLOTS * GROUP, BLK), F32),
                pltpu.VMEM((SLOTS * GROUP, HD), F32),
            ],
            (VMEM, SMEM),
        )(got, kv_pool)

    def gather(places, backs):
        return call(
            functools.partial(gather_kernel, cap),
            shape(ROWS, 16, HD),
            [VMEM, VMEM],
            [pltpu.VMEM((ROWS * 16, HD), F32)],
        )(jnp.concatenate(places, axis=1), jnp.concatenate(backs, axis=0))

    def rounds(count):
        places, backs = [place], [back]
        for k in range(1, count):
            out, more = pack(rows, k * cap)
            places.append(more)
            backs.append(along_z(attend(along_z(out))[0]))
        return gather(places, backs)

    fanned = call(
        fan_kernel,
        shape(ROWS, 16, HD),
        [HBM, HBM, HBM],
        [
            pltpu.VMEM((1, TP * WIDE), BF16),
            pltpu.SMEM((MAXB, TP), jnp.int32),
            pltpu.SMEM((TP,), jnp.int32),
            pltpu.SemaphoreType.DMA((3,)),
        ],
        limit=60 << 20,
    )(queries, block_table.T, lengths)
    rows = over_plane(fanned)
    out, place = pack(rows, 0)
    got = along_z(out)
    got, place, rows, kv_pool = lax.optimization_barrier((got, place, rows, kv_pool))
    back, over = attend(got)
    back = along_z(back)
    back, place, rows, over, kv_pool = lax.optimization_barrier((back, place, rows, over, kv_pool))
    mixed = gather([place], [back])
    mixed = lax.switch(
        over[0], [lambda: mixed, lambda: rounds(2), lambda: rounds(-(-SLOTS // cap))]
    )
    return call(finish_kernel, shape(1, TP * WIDE), [VMEM])(over_plane(mixed))


def solution(mesh):
    fine = Mesh(mesh.devices.reshape(-1, NY, TP // 2, 2), ("z", "y", "x", "c"))
    own = ("z", "y", "x", "c")
    return jax.shard_map(
        functools.partial(per_device, 7),
        mesh=fine,
        in_specs=(
            P(own, None),
            P(None, ("z", "y"), None, ("x", "c")),
            P(("z", "y"), None),
            P(("z", "y")),
        ),
        out_specs=P(own, None),
        check_vma=False,
    )
```

```python
import functools
import math

import jax
import jax.numpy as jnp
from jax import lax
from jax.experimental import pallas as pl
from jax.experimental.pallas import tpu as pltpu
from jax.sharding import Mesh, PartitionSpec as P

HD = 128
NY = 4
TP = 8
GROUP = 8
MAXB = 4
BLK = 256
SLOTS = 32
ROWS = NY * TP
WIDE = GROUP * HD
NEG = -1e30
F32 = jnp.float32
BF16 = jnp.bfloat16


def dot(a, b, dims):
    return lax.dot_general(a, b, (dims, ((), ())), preferred_element_type=F32)


def split(x):
    hi = x.astype(BF16).astype(F32)
    mid = (x - hi).astype(BF16).astype(F32)
    return hi, mid, x - hi - mid


def lanes(shape):
    return lax.broadcasted_iota(jnp.int32, shape, len(shape) - 1)


def fan_kernel(q_hbm, table_hbm, len_hbm, out_ref, q_ref, table_ref, len_ref, sems):
    copies = [
        pltpu.make_async_copy(q_hbm, q_ref, sems.at[0]),
        pltpu.make_async_copy(table_hbm, table_ref, sems.at[1]),
        pltpu.make_async_copy(len_hbm, len_ref, sems.at[2]),
    ]
    for copy in copies:
        copy.start()
    for copy in copies:
        copy.wait()
    t = lax.axis_index("x") * 2 + lax.axis_index("c")
    lane = lanes((TP, GROUP, HD))
    extra = jnp.zeros((TP, GROUP, HD), F32)
    for b in range(MAXB):
        slot = table_ref[b, t]
        extra = jnp.where(lane == b, (slot // SLOTS).astype(F32), extra)
        extra = jnp.where(lane == MAXB + b, (slot % SLOTS).astype(F32), extra)
    length = len_ref[t]
    extra = jnp.where(lane == 8, (length // SLOTS).astype(F32), extra)
    extra = jnp.where(lane == 9, (length % SLOTS).astype(F32), extra)
    q = q_ref[...].astype(F32)
    heads = jnp.concatenate([q[:, h * HD : (h + 1) * HD] for h in range(TP * GROUP)], axis=0)
    both = jnp.concatenate([heads.reshape(TP, GROUP, HD), extra], axis=1).astype(BF16)
    for y in range(NY):
        out_ref[y * TP : (y + 1) * TP] = both


def pack_kernel(cap, skip, a_ref, kv_hbm, out_ref, map_ref, scr):
    y = lax.axis_index("y").astype(F32)
    targets = out_ref.shape[0]
    tall = cap + 1
    scr[...] = a_ref[...].reshape(ROWS * 16, HD).astype(F32)
    query = jnp.concatenate(
        [scr[pl.ds(g, ROWS, stride=16), :] for g in range(GROUP)], axis=1
    ).astype(BF16)
    extra = scr[pl.ds(GROUP, ROWS, stride=16), :]
    pool = jnp.concatenate([extra[:, b : b + 1] for b in range(MAXB)], axis=0)
    slot = jnp.concatenate([extra[:, MAXB + b : MAXB + b + 1] for b in range(MAXB)], axis=0)
    length = extra[:, 8:9] * SLOTS + extra[:, 9:10]
    filled = jnp.concatenate([length - b * BLK for b in range(MAXB)], axis=0)
    filled = jnp.clip(filled, 0.0, float(BLK))
    dest = jnp.floor(pool * (1.0 / NY))
    valid = (pool - dest * NY == y) & (filled > 0.0)
    entries = MAXB * ROWS
    lane = lanes((entries, HD))
    member = jnp.where((lane.astype(F32) == dest) & valid, 1.0, 0.0)
    earlier = jnp.where(
        lax.broadcasted_iota(jnp.int32, (entries, entries), 0) > lanes((entries, entries)), 1.0, 0.0
    ).astype(BF16)
    before = dot(earlier, member.astype(BF16), ((1,), (0,)))
    rank = jnp.sum(before * member, axis=1, keepdims=True)
    most = jnp.max(jnp.sum(member, axis=0, keepdims=True))
    rank = rank - skip
    fits = valid & (rank >= 0.0) & (rank < cap)
    column = lanes((entries, targets)).astype(F32)
    place = jnp.where(column == jnp.where(fits, dest * tall + rank, -1.0), 1.0, 0.0).astype(BF16)
    last = jnp.where(column == jnp.where(fits, dest * tall + cap, -1.0), 1.0, 0.0).astype(BF16)
    map_ref[...] = place
    mine = jnp.where(lane % 2 == 0, slot + 1.0, filled)
    mine = jnp.where((lane // 2).astype(F32) == rank, mine, 0.0).astype(BF16)
    four = jnp.concatenate([query] * MAXB, axis=0)
    out_ref[...] = dot(place, four, ((0,), (0,))).astype(BF16)
    numbers = dot(last, mine, ((0,), (0,)))
    numbers = jnp.where(lanes((targets, HD)) == 2 * cap, most, numbers)
    final = lax.broadcasted_iota(jnp.int32, (targets, HD), 0) % tall == cap
    head = out_ref[:, :HD].astype(F32)
    out_ref[:, :HD] = jnp.where(final, numbers, head).astype(BF16)


def own_lanes(x, tall, width):
    groups = x.shape[0] // tall
    x = x.astype(F32).reshape(groups, tall, HD)
    last = jnp.broadcast_to(x[:, tall - 1 : tall, :], (groups, tall, HD))
    row = lax.broadcasted_iota(jnp.int32, (groups, tall, HD), 1)
    mine = (lanes((groups, tall, HD)) // width == row) & (row < tall - 1)
    return jnp.where(mine, last, 0.0).reshape(groups * tall, HD)


def attend_kernel(cap, b_ref, kv_ref, out_ref, most_ref, q_scr, f_scr, s_scr, p_scr, o_scr):
    targets = b_ref.shape[0]
    tall = cap + 1
    numbers = b_ref[:, :HD]
    lane = lanes((targets, HD))
    row = lax.broadcasted_iota(jnp.int32, (targets, HD), 0)
    most = jnp.max(
        jnp.where((row % tall == cap) & (lane == 2 * cap), numbers.astype(F32), 0.0)
    )
    most_ref[0] = jnp.where(most > 2 * cap, 2, jnp.where(most > cap, 1, 0))
    own = own_lanes(numbers, tall, 2)
    slot = jnp.sum(jnp.where(lane % 2 == 0, own, 0.0), axis=1, keepdims=True) - 1.0
    filled = jnp.sum(jnp.where(lane % 2 == 1, own, 0.0), axis=1, keepdims=True)
    place = jnp.where(lanes((targets, SLOTS)).astype(F32) == slot, 1.0, 0.0).astype(BF16)
    got = dot(place, b_ref[...], ((0,), (0,)))
    filled = jnp.broadcast_to(filled, (targets, HD)).astype(BF16)
    filled = dot(place, filled, ((0,), (0,)))
    for g in range(GROUP):
        rows = pl.ds(g, SLOTS, stride=GROUP)
        q_scr[rows, :] = got[:, g * HD : (g + 1) * HD]
        f_scr[rows, :] = filled
    for s in range(SLOTS):
        rows = slice(s * GROUP, (s + 1) * GROUP)
        s_scr[rows, :] = dot(q_scr[rows, :].astype(BF16), kv_ref[0, s], ((1,), (1,)))
    scores = s_scr[...] * (1.0 / math.sqrt(HD))
    mask = lanes((SLOTS * GROUP, BLK)).astype(F32) < f_scr[:, 0:1]
    scores = jnp.where(mask, scores, NEG)
    peak = jnp.max(scores, axis=1, keepdims=True)
    expo = jnp.where(mask, jnp.exp(scores - peak), 0.0)
    total = jnp.sum(expo, axis=1, keepdims=True)
    used = total > 0.0
    total = jnp.where(used, total, 1.0)
    p_scr[...] = expo
    for s in range(SLOTS):
        rows = slice(s * GROUP, (s + 1) * GROUP)
        o_scr[rows, :] = dot(p_scr[rows, :].astype(BF16), kv_ref[1, s], ((1,), (0,)))
    o_scr[...] = o_scr[...] / total
    level = jnp.where(used, peak + jnp.log(total), NEG)
    f_scr[...] = jnp.broadcast_to(level, (SLOTS * GROUP, HD))
    lane = lanes((SLOTS, HD)) % 16
    coarse = jnp.zeros((SLOTS, HD), F32)
    fine = jnp.zeros((SLOTS, HD), F32)
    parts = []
    for g in range(GROUP):
        rows = pl.ds(g, SLOTS, stride=GROUP)
        parts.append(o_scr[rows, :])
        hi, mid, lo = split(f_scr[rows, :])
        coarse = jnp.where(lane == 2 * g, hi, jnp.where(lane == 2 * g + 1, mid, coarse))
        fine = jnp.where(lane == 2 * g, lo, fine)
    back = jnp.concatenate(parts, axis=1).astype(BF16)
    out_ref[...] = dot(place, back, ((1,), (0,))).astype(BF16)
    final = row % tall == cap
    lane = lanes((targets, HD))
    for k, part in enumerate((coarse, fine)):
        each = dot(place, part.astype(BF16), ((1,), (0,)))
        each = jnp.where(lane // 16 == row % tall, each, 0.0).reshape(targets // tall, tall, HD)
        both = jnp.broadcast_to(jnp.sum(each, axis=1, keepdims=True), each.shape)
        spot = slice(k * HD, (k + 1) * HD)
        head = out_ref[:, spot].astype(F32)
        out_ref[:, spot] = jnp.where(final, both.reshape(targets, HD), head).astype(BF16)


def gather_kernel(cap, map_ref, c_ref, out_ref, scr):
    tall = cap + 1
    coarse = own_lanes(c_ref[:, :HD], tall, 16).astype(BF16)
    fine = own_lanes(c_ref[:, HD : 2 * HD], tall, 16).astype(BF16)
    pick = lax.broadcasted_iota(jnp.int32, (HD, HD), 0) % 16 // 2 == lanes((HD, HD))
    pick = jnp.where(pick, 1.0, 0.0).astype(BF16)
    got, ok, levels = [], [], []
    for b in range(MAXB):
        place = map_ref[b * ROWS : (b + 1) * ROWS, :]
        got.append(dot(place, c_ref[...], ((1,), (0,))))
        ok.append(jnp.sum(place.astype(F32), axis=1, keepdims=True) > 0.0)
        level = 0.0
        for part in (coarse, fine):
            part = dot(place, part, ((1,), (0,))).astype(BF16)
            level = level + dot(part, pick, ((1,), (0,)))
        levels.append(level)
    lane = lanes((ROWS, HD))
    top = functools.reduce(
        jnp.maximum, [jnp.where(o, level, NEG) for o, level in zip(ok, levels)]
    )
    factor = [jnp.where(o, jnp.exp(level - top), 0.0) for o, level in zip(ok, levels)]
    total = functools.reduce(jnp.add, factor)
    any_ok = total > 0.0
    total = jnp.where(any_ok, total, 1.0)
    three = split(jnp.where(any_ok, top + jnp.log(total), NEG))
    factor = [f / total for f in factor]
    for g in range(GROUP):
        mixed = functools.reduce(
            jnp.add,
            [factor[b][:, g : g + 1] * got[b][:, g * HD : (g + 1) * HD] for b in range(MAXB)],
        )
        scr[pl.ds(g, ROWS, stride=16), :] = mixed
        hi, mid, lo = [part[:, g : g + 1] for part in three]
        scr[pl.ds(GROUP + g, ROWS, stride=16), :] = jnp.where(
            lane == 0, hi, jnp.where(lane == 1, mid, jnp.where(lane == 2, lo, 0.0))
        )
    out_ref[...] = scr[...].reshape(ROWS, 16, HD).astype(BF16)


def finish_kernel(d_ref, out_ref):
    parts, level = [], []
    for y in range(NY):
        x = d_ref[y * TP : (y + 1) * TP].astype(F32)
        parts.append(x[:, :GROUP, :])
        level.append(jnp.sum(x[:, GROUP:, :], axis=2, keepdims=True))
    top = functools.reduce(jnp.maximum, level)
    factor = [jnp.exp(one - top) for one in level]
    total = functools.reduce(jnp.add, factor)
    mixed = functools.reduce(jnp.add, [f * p for f, p in zip(factor, parts)])
    result = (mixed / total).reshape(TP * GROUP, HD)
    out_ref[...] = jnp.concatenate(
        [result[h : h + 1, :] for h in range(TP * GROUP)], axis=1
    ).astype(BF16)


SMEM = pl.BlockSpec(memory_space=pltpu.SMEM)
VMEM = pl.BlockSpec(memory_space=pltpu.VMEM)
HBM = pl.BlockSpec(memory_space=pltpu.HBM)


def call(kernel, out, ins, scratch=(), outs=VMEM, limit=24 << 20):
    return pl.pallas_call(
        kernel,
        out_shape=out,
        in_specs=ins,
        out_specs=outs,
        scratch_shapes=scratch,
        compiler_params=pltpu.CompilerParams(vmem_limit_bytes=limit),
    )


def shape(*dims):
    return jax.ShapeDtypeStruct(dims, BF16)


def per_device(cap, queries, kv_pool, block_table, lengths):
    nz = lax.axis_size("z")
    targets = nz * (cap + 1)

    def over_plane(x):
        return lax.all_to_all(x, ("y", "x", "c"), 0, 0, tiled=True)

    def along_z(x):
        x = lax.all_to_all(x.reshape(nz, -1, WIDE), "z", 0, 0, tiled=True)
        return x.reshape(-1, WIDE)

    def pack(rows, skip):
        return call(
            functools.partial(pack_kernel, cap, skip),
            (shape(targets, WIDE), shape(MAXB * ROWS, targets)),
            [VMEM, HBM],
            [pltpu.VMEM((ROWS * 16, HD), F32)],
            (VMEM, VMEM),
        )(rows, kv_pool)

    def attend(got):
        return call(
            functools.partial(attend_kernel, cap),
            (shape(targets, WIDE), pltpu.SMEM((1,), jnp.int32)),
            [VMEM, VMEM],
            [
                pltpu.VMEM((SLOTS * GROUP, HD), F32),
                pltpu.VMEM((SLOTS * GROUP, HD), F32),
                pltpu.VMEM((SLOTS * GROUP, BLK), F32),
                pltpu.VMEM((SLOTS * GROUP, BLK), F32),
                pltpu.VMEM((SLOTS * GROUP, HD), F32),
            ],
            (VMEM, SMEM),
        )(got, kv_pool)

    def gather(places, backs):
        return call(
            functools.partial(gather_kernel, cap),
            shape(ROWS, 16, HD),
            [VMEM, VMEM],
            [pltpu.VMEM((ROWS * 16, HD), F32)],
        )(jnp.concatenate(places, axis=1), jnp.concatenate(backs, axis=0))

    def rounds(count):
        places, backs = [place], [back]
        for k in range(1, count):
            out, more = pack(rows, k * cap)
            places.append(more)
            backs.append(along_z(attend(along_z(out))[0]))
        return gather(places, backs)

    fanned = call(
        fan_kernel,
        shape(ROWS, 16, HD),
        [HBM, HBM, HBM],
        [
            pltpu.VMEM((1, TP * WIDE), BF16),
            pltpu.SMEM((MAXB, TP), jnp.int32),
            pltpu.SMEM((TP,), jnp.int32),
            pltpu.SemaphoreType.DMA((3,)),
        ],
    )(*(pltpu.with_memory_space_constraint(x, pltpu.HBM) for x in (queries, block_table.T, lengths)))
    rows = over_plane(fanned)
    out, place = pack(rows, 0)
    got = along_z(out)
    got, place, rows, kv_pool = lax.optimization_barrier((got, place, rows, kv_pool))
    back, over = attend(got)
    back = along_z(back)
    back, place, rows, over, kv_pool = lax.optimization_barrier((back, place, rows, over, kv_pool))
    mixed = gather([place], [back])
    mixed = lax.switch(
        over[0], [lambda: mixed, lambda: rounds(2), lambda: rounds(-(-SLOTS // cap))]
    )
    return call(finish_kernel, shape(1, TP * WIDE), [VMEM])(over_plane(mixed))


def solution(mesh):
    fine = Mesh(mesh.devices.reshape(-1, NY, TP // 2, 2), ("z", "y", "x", "c"))
    own = ("z", "y", "x", "c")
    return jax.shard_map(
        functools.partial(per_device, 7),
        mesh=fine,
        in_specs=(
            P(own, None),
            P(None, ("z", "y"), None, ("x", "c")),
            P(("z", "y"), None),
            P(("z", "y")),
        ),
        out_specs=P(own, None),
        check_vma=False,
    )
```

```python
import functools
import math

import jax
import jax.numpy as jnp
from jax import lax
from jax.experimental import pallas as pl
from jax.experimental.pallas import tpu as pltpu
from jax.sharding import Mesh, PartitionSpec as P

HD = 128
NY = 4
TP = 8
GROUP = 8
MAXB = 4
BLK = 256
SLOTS = 32
ROWS = NY * TP
WIDE = GROUP * HD
NEG = -1e30
F32 = jnp.float32
BF16 = jnp.bfloat16


def dot(a, b, dims):
    return lax.dot_general(a, b, (dims, ((), ())), preferred_element_type=F32)


def split(x):
    hi = x.astype(BF16).astype(F32)
    mid = (x - hi).astype(BF16).astype(F32)
    return hi, mid, x - hi - mid


def lanes(shape):
    return lax.broadcasted_iota(jnp.int32, shape, len(shape) - 1)


def up(shape):
    return lax.broadcasted_iota(jnp.int32, shape, 0)


def fan_kernel(q_hbm, table_hbm, len_hbm, out_ref, q_ref, table_ref, len_ref, sems):
    copies = [
        pltpu.make_async_copy(q_hbm, q_ref, sems.at[0]),
        pltpu.make_async_copy(table_hbm, table_ref, sems.at[1]),
        pltpu.make_async_copy(len_hbm, len_ref, sems.at[2]),
    ]
    for copy in copies:
        copy.start()
    for copy in copies:
        copy.wait()
    t = lax.axis_index("x") * 2 + lax.axis_index("c")
    lane = lanes((TP, GROUP, HD))
    extra = jnp.zeros((TP, GROUP, HD), F32)
    for b in range(MAXB):
        slot = table_ref[b, t]
        extra = jnp.where(lane == b, (slot // SLOTS).astype(F32), extra)
        extra = jnp.where(lane == MAXB + b, (slot % SLOTS).astype(F32), extra)
    length = len_ref[t]
    extra = jnp.where(lane == 8, (length // SLOTS).astype(F32), extra)
    extra = jnp.where(lane == 9, (length % SLOTS).astype(F32), extra)
    q = q_ref[...].astype(F32)
    heads = jnp.concatenate([q[:, h * HD : (h + 1) * HD] for h in range(TP * GROUP)], axis=0)
    both = jnp.concatenate([heads.reshape(TP, GROUP, HD), extra], axis=1).astype(BF16)
    for y in range(NY):
        out_ref[y * TP : (y + 1) * TP] = both


def pack_kernel(cap, skip, a_ref, kv_hbm, out_ref, map_ref, scr):
    y = lax.axis_index("y").astype(F32)
    targets = out_ref.shape[0]
    tall = cap + 1
    scr[...] = a_ref[...].reshape(ROWS * 16, HD).astype(F32)
    query = jnp.concatenate(
        [scr[pl.ds(g, ROWS, stride=16), :] for g in range(GROUP)], axis=1
    ).astype(BF16)
    extra = scr[pl.ds(GROUP, ROWS, stride=16), :]
    extra = extra.T
    pool = jnp.concatenate([extra[b : b + 1] for b in range(MAXB)], axis=1)
    slot = jnp.concatenate([extra[MAXB + b : MAXB + b + 1] for b in range(MAXB)], axis=1)
    length = extra[8:9] * SLOTS + extra[9:10]
    filled = jnp.concatenate([length - b * BLK for b in range(MAXB)], axis=1)
    filled = jnp.clip(filled, 0.0, float(BLK))
    dest = jnp.floor(pool * (1.0 / NY))
    valid = (pool - dest * NY == y) & (filled > 0.0)
    entries = MAXB * ROWS
    planes = targets // tall
    member = jnp.where((up((planes, entries)).astype(F32) == dest) & valid, 1.0, 0.0)
    earlier = jnp.where(up((entries, entries)) < lanes((entries, entries)), 1.0, 0.0)
    before = dot(member.astype(BF16), earlier.astype(BF16), ((1,), (0,)))
    rank = jnp.sum(before * member, axis=0, keepdims=True)
    most = jnp.max(jnp.sum(member, axis=1, keepdims=True), axis=0, keepdims=True)
    rank = rank - skip
    fits = valid & (rank >= 0.0) & (rank < cap)
    spot = up((targets, entries)).astype(F32)
    place = jnp.where(spot == jnp.where(fits, dest * tall + rank, -1.0), 1.0, 0.0)
    last = jnp.where(spot == jnp.where(fits, dest * tall + cap, -1.0), 1.0, 0.0).astype(BF16)
    side = up((HD, entries))
    mine = jnp.where(side % 2 == 0, slot + 1.0, filled)
    mine = jnp.where((side // 2).astype(F32) == rank, mine, 0.0).astype(BF16)
    four = jnp.concatenate([query] * MAXB, axis=0)
    out = dot(place.astype(BF16), four, ((1,), (0,)))
    out_ref[:, HD:] = out[:, HD:].astype(BF16)
    numbers = dot(last, mine, ((1,), (1,)))
    numbers = jnp.where(lanes((targets, HD)) == 2 * cap, most, numbers)
    final = up((targets, HD)) % tall == cap
    out_ref[:, :HD] = jnp.where(final, numbers, out[:, :HD]).astype(BF16)
    map_ref[...] = place.T.astype(BF16)


def own_lanes(x, tall, width):
    groups = x.shape[0] // tall
    x = x.astype(F32).reshape(groups, tall, HD)
    last = jnp.broadcast_to(x[:, tall - 1 : tall, :], (groups, tall, HD))
    row = lax.broadcasted_iota(jnp.int32, (groups, tall, HD), 1)
    mine = (lanes((groups, tall, HD)) // width == row) & (row < tall - 1)
    return jnp.where(mine, last, 0.0).reshape(groups * tall, HD)


def attend_kernel(cap, b_ref, kv_ref, out_ref, most_ref, q_scr, f_scr, s_scr, p_scr, o_scr):
    targets = b_ref.shape[0]
    tall = cap + 1
    numbers = b_ref[:, :HD]
    lane = lanes((targets, HD))
    row = lax.broadcasted_iota(jnp.int32, (targets, HD), 0)
    most = jnp.max(
        jnp.where((row % tall == cap) & (lane == 2 * cap), numbers.astype(F32), 0.0)
    )
    most_ref[0] = jnp.where(most > 2 * cap, 2, jnp.where(most > cap, 1, 0))
    own = own_lanes(numbers, tall, 2).astype(BF16)
    odd = jnp.where(lanes((8, HD)) % 2 == up((8, HD)), 1.0, 0.0).astype(BF16)
    pair = dot(odd, own, ((1,), (1,)))
    place = jnp.where(up((SLOTS, targets)).astype(F32) == pair[0:1] - 1.0, 1.0, 0.0)
    filled = jnp.sum(place * pair[1:2], axis=1, keepdims=True)
    filled = jnp.broadcast_to(filled, (SLOTS, HD))
    back_place = place.T.astype(BF16)
    got = dot(place.astype(BF16), b_ref[...], ((1,), (0,)))
    for g in range(GROUP):
        rows = pl.ds(g, SLOTS, stride=GROUP)
        q_scr[rows, :] = got[:, g * HD : (g + 1) * HD]
        f_scr[rows, :] = filled
    for s in range(SLOTS):
        rows = slice(s * GROUP, (s + 1) * GROUP)
        s_scr[rows, :] = dot(q_scr[rows, :].astype(BF16), kv_ref[0, s], ((1,), (1,)))
    scores = s_scr[...] * (1.0 / math.sqrt(HD))
    mask = lanes((SLOTS * GROUP, BLK)).astype(F32) < f_scr[:, 0:1]
    scores = jnp.where(mask, scores, NEG)
    peak = jnp.max(scores, axis=1, keepdims=True)
    expo = jnp.where(mask, jnp.exp(scores - peak), 0.0)
    total = jnp.sum(expo, axis=1, keepdims=True)
    used = total > 0.0
    total = jnp.where(used, total, 1.0)
    p_scr[...] = expo
    for s in range(SLOTS):
        rows = slice(s * GROUP, (s + 1) * GROUP)
        o_scr[rows, :] = dot(p_scr[rows, :].astype(BF16), kv_ref[1, s], ((1,), (0,)))
    o_scr[...] = o_scr[...] / total
    level = jnp.where(used, peak + jnp.log(total), NEG)
    f_scr[...] = jnp.broadcast_to(level, (SLOTS * GROUP, HD))
    lane = lanes((SLOTS, HD)) % 16
    coarse = jnp.zeros((SLOTS, HD), F32)
    fine = jnp.zeros((SLOTS, HD), F32)
    parts = []
    for g in range(GROUP):
        rows = pl.ds(g, SLOTS, stride=GROUP)
        parts.append(o_scr[rows, :])
        hi, mid, lo = split(f_scr[rows, :])
        coarse = jnp.where(lane == 2 * g, hi, jnp.where(lane == 2 * g + 1, mid, coarse))
        fine = jnp.where(lane == 2 * g, lo, fine)
    back = jnp.concatenate(parts, axis=1).astype(BF16)
    out = dot(back_place, back, ((1,), (0,)))
    out_ref[:, 2 * HD :] = out[:, 2 * HD :].astype(BF16)
    final = row % tall == cap
    lane = lanes((targets, HD))
    for k, part in enumerate((coarse, fine)):
        each = dot(back_place, part.astype(BF16), ((1,), (0,)))
        each = jnp.where(lane // 16 == row % tall, each, 0.0).reshape(targets // tall, tall, HD)
        both = jnp.broadcast_to(jnp.sum(each, axis=1, keepdims=True), each.shape)
        spot = slice(k * HD, (k + 1) * HD)
        out_ref[:, spot] = jnp.where(final, both.reshape(targets, HD), out[:, spot]).astype(BF16)


def gather_kernel(cap, map_ref, c_ref, out_ref, scr):
    tall = cap + 1
    coarse = own_lanes(c_ref[:, :HD], tall, 16).astype(BF16)
    fine = own_lanes(c_ref[:, HD : 2 * HD], tall, 16).astype(BF16)
    pick = lax.broadcasted_iota(jnp.int32, (HD, HD), 0) % 16 // 2 == lanes((HD, HD))
    pick = jnp.where(pick, 1.0, 0.0).astype(BF16)
    place = map_ref[...]
    got = dot(place, c_ref[...], ((1,), (0,)))
    level = 0.0
    for part in (coarse, fine):
        part = dot(place, part, ((1,), (0,))).astype(BF16)
        level = level + dot(part, pick, ((1,), (0,)))
    found = jnp.sum(place.astype(F32), axis=1, keepdims=True) > 0.0
    level = jnp.where(found, level, NEG)
    blocks = [slice(b * ROWS, (b + 1) * ROWS) for b in range(MAXB)]
    levels = [level[b] for b in blocks]
    ok = [found[b] for b in blocks]
    got = [got[b] for b in blocks]
    lane = lanes((ROWS, HD))
    top = functools.reduce(jnp.maximum, levels)
    factor = [jnp.where(o, jnp.exp(level - top), 0.0) for o, level in zip(ok, levels)]
    total = functools.reduce(jnp.add, factor)
    any_ok = total > 0.0
    total = jnp.where(any_ok, total, 1.0)
    three = split(jnp.where(any_ok, top + jnp.log(total), NEG))
    factor = [f / total for f in factor]
    for g in range(GROUP):
        mixed = functools.reduce(
            jnp.add,
            [factor[b][:, g : g + 1] * got[b][:, g * HD : (g + 1) * HD] for b in range(MAXB)],
        )
        scr[pl.ds(g, ROWS, stride=16), :] = mixed
        hi, mid, lo = [part[:, g : g + 1] for part in three]
        scr[pl.ds(GROUP + g, ROWS, stride=16), :] = jnp.where(
            lane == 0, hi, jnp.where(lane == 1, mid, jnp.where(lane == 2, lo, 0.0))
        )
    out_ref[...] = scr[...].reshape(ROWS, 16, HD).astype(BF16)


def finish_kernel(d_ref, out_ref):
    parts, level = [], []
    for y in range(NY):
        x = d_ref[y * TP : (y + 1) * TP].astype(F32)
        parts.append(x[:, :GROUP, :])
        level.append(jnp.sum(x[:, GROUP:, :], axis=2, keepdims=True))
    top = functools.reduce(jnp.maximum, level)
    factor = [jnp.exp(one - top) for one in level]
    total = functools.reduce(jnp.add, factor)
    mixed = functools.reduce(jnp.add, [f * p for f, p in zip(factor, parts)])
    result = (mixed / total).reshape(TP * GROUP, HD)
    out_ref[...] = jnp.concatenate(
        [result[h : h + 1, :] for h in range(TP * GROUP)], axis=1
    ).astype(BF16)


SMEM = pl.BlockSpec(memory_space=pltpu.SMEM)
VMEM = pl.BlockSpec(memory_space=pltpu.VMEM)
HBM = pl.BlockSpec(memory_space=pltpu.HBM)


def call(kernel, out, ins, scratch=(), outs=VMEM, limit=24 << 20):
    return pl.pallas_call(
        kernel,
        out_shape=out,
        in_specs=ins,
        out_specs=outs,
        scratch_shapes=scratch,
        compiler_params=pltpu.CompilerParams(vmem_limit_bytes=limit),
    )


def shape(*dims):
    return jax.ShapeDtypeStruct(dims, BF16)


def per_device(cap, queries, kv_pool, block_table, lengths):
    nz = lax.axis_size("z")
    targets = nz * (cap + 1)

    def over_plane(x):
        return lax.all_to_all(x, ("y", "x", "c"), 0, 0, tiled=True)

    def along_z(x):
        x = lax.all_to_all(x.reshape(nz, -1, WIDE), "z", 0, 0, tiled=True)
        return x.reshape(-1, WIDE)

    def pack(rows, skip):
        return call(
            functools.partial(pack_kernel, cap, skip),
            (shape(targets, WIDE), shape(MAXB * ROWS, targets)),
            [VMEM, HBM],
            [pltpu.VMEM((ROWS * 16, HD), F32)],
            (VMEM, VMEM),
        )(rows, kv_pool)

    def attend(got):
        return call(
            functools.partial(attend_kernel, cap),
            (shape(targets, WIDE), pltpu.SMEM((1,), jnp.int32)),
            [VMEM, VMEM],
            [
                pltpu.VMEM((SLOTS * GROUP, HD), F32),
                pltpu.VMEM((SLOTS * GROUP, HD), F32),
                pltpu.VMEM((SLOTS * GROUP, BLK), F32),
                pltpu.VMEM((SLOTS * GROUP, BLK), F32),
                pltpu.VMEM((SLOTS * GROUP, HD), F32),
            ],
            (VMEM, SMEM),
        )(got, kv_pool)

    def gather(places, backs):
        return call(
            functools.partial(gather_kernel, cap),
            shape(ROWS, 16, HD),
            [VMEM, VMEM],
            [pltpu.VMEM((ROWS * 16, HD), F32)],
        )(jnp.concatenate(places, axis=1), jnp.concatenate(backs, axis=0))

    def rounds(count):
        places, backs = [place], [back]
        for k in range(1, count):
            out, more = pack(rows, k * cap)
            places.append(more)
            backs.append(along_z(attend(along_z(out))[0]))
        return gather(places, backs)

    fanned = call(
        fan_kernel,
        shape(ROWS, 16, HD),
        [HBM, HBM, HBM],
        [
            pltpu.VMEM((1, TP * WIDE), BF16),
            pltpu.SMEM((MAXB, TP), jnp.int32),
            pltpu.SMEM((TP,), jnp.int32),
            pltpu.SemaphoreType.DMA((3,)),
        ],
    )(*(pltpu.with_memory_space_constraint(x, pltpu.HBM) for x in (queries, block_table.T, lengths)))
    rows = over_plane(fanned)
    out, place = pack(rows, 0)
    got = along_z(out)
    got, place, rows, kv_pool = lax.optimization_barrier((got, place, rows, kv_pool))
    back, over = attend(got)
    back = along_z(back)
    back, place, rows, over, kv_pool = lax.optimization_barrier((back, place, rows, over, kv_pool))
    mixed = gather([place], [back])
    mixed = lax.switch(
        over[0], [lambda: mixed, lambda: rounds(2), lambda: rounds(-(-SLOTS // cap))]
    )
    return call(finish_kernel, shape(1, TP * WIDE), [VMEM])(over_plane(mixed))


def solution(mesh):
    fine = Mesh(mesh.devices.reshape(-1, NY, TP // 2, 2), ("z", "y", "x", "c"))
    own = ("z", "y", "x", "c")
    return jax.shard_map(
        functools.partial(per_device, 7),
        mesh=fine,
        in_specs=(
            P(own, None),
            P(None, ("z", "y"), None, ("x", "c")),
            P(("z", "y"), None),
            P(("z", "y")),
        ),
        out_specs=P(own, None),
        check_vma=False,
    )
```

```python
import functools
import math

import jax
import jax.numpy as jnp
from jax import lax
from jax.experimental import pallas as pl
from jax.experimental.pallas import tpu as pltpu
from jax.sharding import Mesh, PartitionSpec as P

HD = 128
NY = 4
TP = 8
GROUP = 8
MAXB = 4
BLK = 256
SLOTS = 32
ROWS = NY * TP
WIDE = GROUP * HD
HALF = TP * GROUP // 2
NEG = -1e30
F32 = jnp.float32
BF16 = jnp.bfloat16


def dot(a, b, dims):
    return lax.dot_general(a, b, (dims, ((), ())), preferred_element_type=F32)


def split(x):
    hi = x.astype(BF16).astype(F32)
    mid = (x - hi).astype(BF16).astype(F32)
    return hi, mid, x - hi - mid


def lanes(shape):
    return lax.broadcasted_iota(jnp.int32, shape, len(shape) - 1)


def up(shape):
    return lax.broadcasted_iota(jnp.int32, shape, 0)


def fan_kernel(q_hbm, table_hbm, len_hbm, out_ref, q_ref, table_ref, len_ref, sems):
    copies = [
        pltpu.make_async_copy(q_hbm, q_ref, sems.at[0]),
        pltpu.make_async_copy(table_hbm, table_ref, sems.at[1]),
        pltpu.make_async_copy(len_hbm, len_ref, sems.at[2]),
    ]
    for copy in copies:
        copy.start()
    for copy in copies:
        copy.wait()
    t = lax.axis_index("x") * 2 + lax.axis_index("c")
    lane = lanes((TP, GROUP, HD))
    extra = jnp.zeros((TP, GROUP, HD), F32)
    for b in range(MAXB):
        slot = table_ref[b, t]
        extra = jnp.where(lane == b, (slot // SLOTS).astype(F32), extra)
        extra = jnp.where(lane == MAXB + b, (slot % SLOTS).astype(F32), extra)
    length = len_ref[t]
    extra = jnp.where(lane == 8, (length // SLOTS).astype(F32), extra)
    extra = jnp.where(lane == 9, (length % SLOTS).astype(F32), extra)
    q = q_ref[...].astype(F32)
    heads = jnp.concatenate([q[:, h * HD : (h + 1) * HD] for h in range(TP * GROUP)], axis=0)
    heads = jnp.concatenate([heads[HALF:], heads[:HALF]], axis=0)
    both = jnp.concatenate([heads.reshape(TP, GROUP, HD), extra], axis=1).astype(BF16)
    for y in range(NY):
        out_ref[y * TP : (y + 1) * TP] = both


def pack_kernel(cap, skip, a_ref, kv_hbm, out_ref, map_ref, scr):
    y = lax.axis_index("y").astype(F32)
    targets = out_ref.shape[0]
    tall = cap + 1
    scr[...] = a_ref[...].reshape(ROWS * 16, HD).astype(F32)
    query = jnp.concatenate(
        [scr[pl.ds(g, ROWS, stride=16), :] for g in range(GROUP)], axis=1
    ).astype(BF16)
    extra = scr[pl.ds(GROUP, ROWS, stride=16), :]
    extra = extra.T
    pool = jnp.concatenate([extra[b : b + 1] for b in range(MAXB)], axis=1)
    slot = jnp.concatenate([extra[MAXB + b : MAXB + b + 1] for b in range(MAXB)], axis=1)
    length = extra[8:9] * SLOTS + extra[9:10]
    filled = jnp.concatenate([length - b * BLK for b in range(MAXB)], axis=1)
    filled = jnp.clip(filled, 0.0, float(BLK))
    dest = jnp.floor(pool * (1.0 / NY))
    valid = (pool - dest * NY == y) & (filled > 0.0)
    entries = MAXB * ROWS
    planes = targets // tall
    dest = jnp.where(dest < planes // 2, dest + planes // 2, dest - planes // 2)
    member = jnp.where((up((planes, entries)).astype(F32) == dest) & valid, 1.0, 0.0)
    earlier = jnp.where(up((entries, entries)) < lanes((entries, entries)), 1.0, 0.0)
    before = dot(member.astype(BF16), earlier.astype(BF16), ((1,), (0,)))
    rank = jnp.sum(before * member, axis=0, keepdims=True)
    most = jnp.max(jnp.sum(member, axis=1, keepdims=True), axis=0, keepdims=True)
    rank = rank - skip
    fits = valid & (rank >= 0.0) & (rank < cap)
    spot = up((targets, entries)).astype(F32)
    place = jnp.where(spot == jnp.where(fits, dest * tall + rank, -1.0), 1.0, 0.0)
    last = jnp.where(spot == jnp.where(fits, dest * tall + cap, -1.0), 1.0, 0.0).astype(BF16)
    side = up((HD, entries))
    mine = jnp.where(side % 2 == 0, slot + 1.0, filled)
    mine = jnp.where((side // 2).astype(F32) == rank, mine, 0.0).astype(BF16)
    four = jnp.concatenate([query] * MAXB, axis=0)
    out = dot(place.astype(BF16), four, ((1,), (0,)))
    out_ref[:, HD:] = out[:, HD:].astype(BF16)
    numbers = dot(last, mine, ((1,), (1,)))
    numbers = jnp.where(lanes((targets, HD)) == 2 * cap, most, numbers)
    final = up((targets, HD)) % tall == cap
    out_ref[:, :HD] = jnp.where(final, numbers, out[:, :HD]).astype(BF16)
    map_ref[...] = place.T.astype(BF16)


def own_lanes(x, tall, width):
    groups = x.shape[0] // tall
    x = x.astype(F32).reshape(groups, tall, HD)
    last = jnp.broadcast_to(x[:, tall - 1 : tall, :], (groups, tall, HD))
    row = lax.broadcasted_iota(jnp.int32, (groups, tall, HD), 1)
    mine = (lanes((groups, tall, HD)) // width == row) & (row < tall - 1)
    return jnp.where(mine, last, 0.0).reshape(groups * tall, HD)


def attend_kernel(cap, b_ref, kv_ref, out_ref, most_ref, q_scr, f_scr, s_scr, p_scr, o_scr):
    targets = b_ref.shape[0]
    tall = cap + 1
    numbers = b_ref[:, :HD]
    lane = lanes((targets, HD))
    row = lax.broadcasted_iota(jnp.int32, (targets, HD), 0)
    most = jnp.max(
        jnp.where((row % tall == cap) & (lane == 2 * cap), numbers.astype(F32), 0.0)
    )
    most_ref[0] = jnp.where(most > 2 * cap, 2, jnp.where(most > cap, 1, 0))
    own = own_lanes(numbers, tall, 2).astype(BF16)
    odd = jnp.where(lanes((8, HD)) % 2 == up((8, HD)), 1.0, 0.0).astype(BF16)
    pair = dot(odd, own, ((1,), (1,)))
    place = jnp.where(up((SLOTS, targets)).astype(F32) == pair[0:1] - 1.0, 1.0, 0.0)
    filled = jnp.sum(place * pair[1:2], axis=1, keepdims=True)
    filled = jnp.broadcast_to(filled, (SLOTS, HD))
    back_place = place.T.astype(BF16)
    got = dot(place.astype(BF16), b_ref[...], ((1,), (0,)))
    for g in range(GROUP):
        rows = pl.ds(g, SLOTS, stride=GROUP)
        q_scr[rows, :] = got[:, g * HD : (g + 1) * HD]
        f_scr[rows, :] = filled
    for s in range(SLOTS):
        rows = slice(s * GROUP, (s + 1) * GROUP)
        s_scr[rows, :] = dot(q_scr[rows, :].astype(BF16), kv_ref[0, s], ((1,), (1,)))
    scores = s_scr[...] * (1.0 / math.sqrt(HD))
    mask = lanes((SLOTS * GROUP, BLK)).astype(F32) < f_scr[:, 0:1]
    scores = jnp.where(mask, scores, NEG)
    peak = jnp.max(scores, axis=1, keepdims=True)
    expo = jnp.where(mask, jnp.exp(scores - peak), 0.0)
    total = jnp.sum(expo, axis=1, keepdims=True)
    used = total > 0.0
    total = jnp.where(used, total, 1.0)
    p_scr[...] = expo
    for s in range(SLOTS):
        rows = slice(s * GROUP, (s + 1) * GROUP)
        o_scr[rows, :] = dot(p_scr[rows, :].astype(BF16), kv_ref[1, s], ((1,), (0,)))
    o_scr[...] = o_scr[...] / total
    level = jnp.where(used, peak + jnp.log(total), NEG)
    f_scr[...] = jnp.broadcast_to(level, (SLOTS * GROUP, HD))
    lane = lanes((SLOTS, HD)) % 16
    coarse = jnp.zeros((SLOTS, HD), F32)
    fine = jnp.zeros((SLOTS, HD), F32)
    parts = []
    for g in range(GROUP):
        rows = pl.ds(g, SLOTS, stride=GROUP)
        parts.append(o_scr[rows, :])
        hi, mid, lo = split(f_scr[rows, :])
        coarse = jnp.where(lane == 2 * g, hi, jnp.where(lane == 2 * g + 1, mid, coarse))
        fine = jnp.where(lane == 2 * g, lo, fine)
    back = jnp.concatenate(parts, axis=1).astype(BF16)
    out = dot(back_place, back, ((1,), (0,)))
    out_ref[:, 2 * HD :] = out[:, 2 * HD :].astype(BF16)
    final = row % tall == cap
    lane = lanes((targets, HD))
    for k, part in enumerate((coarse, fine)):
        each = dot(back_place, part.astype(BF16), ((1,), (0,)))
        each = jnp.where(lane // 16 == row % tall, each, 0.0).reshape(targets // tall, tall, HD)
        both = jnp.broadcast_to(jnp.sum(each, axis=1, keepdims=True), each.shape)
        spot = slice(k * HD, (k + 1) * HD)
        out_ref[:, spot] = jnp.where(final, both.reshape(targets, HD), out[:, spot]).astype(BF16)


def gather_kernel(cap, map_ref, c_ref, out_ref, scr):
    tall = cap + 1
    coarse = own_lanes(c_ref[:, :HD], tall, 16).astype(BF16)
    fine = own_lanes(c_ref[:, HD : 2 * HD], tall, 16).astype(BF16)
    pick = lax.broadcasted_iota(jnp.int32, (HD, HD), 0) % 16 // 2 == lanes((HD, HD))
    pick = jnp.where(pick, 1.0, 0.0).astype(BF16)
    place = map_ref[...]
    got = dot(place, c_ref[...], ((1,), (0,)))
    level = 0.0
    for part in (coarse, fine):
        part = dot(place, part, ((1,), (0,))).astype(BF16)
        level = level + dot(part, pick, ((1,), (0,)))
    found = jnp.sum(place.astype(F32), axis=1, keepdims=True) > 0.0
    level = jnp.where(found, level, NEG)
    blocks = [slice(b * ROWS, (b + 1) * ROWS) for b in range(MAXB)]
    levels = [level[b] for b in blocks]
    ok = [found[b] for b in blocks]
    got = [got[b] for b in blocks]
    lane = lanes((ROWS, HD))
    top = functools.reduce(jnp.maximum, levels)
    factor = [jnp.where(o, jnp.exp(level - top), 0.0) for o, level in zip(ok, levels)]
    total = functools.reduce(jnp.add, factor)
    any_ok = total > 0.0
    total = jnp.where(any_ok, total, 1.0)
    three = split(jnp.where(any_ok, top + jnp.log(total), NEG))
    factor = [f / total for f in factor]
    for g in range(GROUP):
        mixed = functools.reduce(
            jnp.add,
            [factor[b][:, g : g + 1] * got[b][:, g * HD : (g + 1) * HD] for b in range(MAXB)],
        )
        scr[pl.ds(g, ROWS, stride=16), :] = mixed
        hi, mid, lo = [part[:, g : g + 1] for part in three]
        scr[pl.ds(GROUP + g, ROWS, stride=16), :] = jnp.where(
            lane == 0, hi, jnp.where(lane == 1, mid, jnp.where(lane == 2, lo, 0.0))
        )
    out_ref[...] = scr[...].reshape(ROWS, 16, HD).astype(BF16)


def finish_kernel(d_ref, out_ref):
    parts, level = [], []
    for y in range(NY):
        x = d_ref[y * TP : (y + 1) * TP].astype(F32)
        parts.append(x[:, :GROUP, :])
        level.append(jnp.sum(x[:, GROUP:, :], axis=2, keepdims=True))
    top = functools.reduce(jnp.maximum, level)
    factor = [jnp.exp(one - top) for one in level]
    total = functools.reduce(jnp.add, factor)
    mixed = functools.reduce(jnp.add, [f * p for f, p in zip(factor, parts)])
    result = (mixed / total).reshape(TP * GROUP, HD)
    result = jnp.concatenate([result[HALF:], result[:HALF]], axis=0)
    out_ref[...] = jnp.concatenate(
        [result[h : h + 1, :] for h in range(TP * GROUP)], axis=1
    ).astype(BF16)


SMEM = pl.BlockSpec(memory_space=pltpu.SMEM)
VMEM = pl.BlockSpec(memory_space=pltpu.VMEM)
HBM = pl.BlockSpec(memory_space=pltpu.HBM)


def call(kernel, out, ins, scratch=(), outs=VMEM, limit=24 << 20):
    return pl.pallas_call(
        kernel,
        out_shape=out,
        in_specs=ins,
        out_specs=outs,
        scratch_shapes=scratch,
        compiler_params=pltpu.CompilerParams(vmem_limit_bytes=limit),
    )


def shape(*dims):
    return jax.ShapeDtypeStruct(dims, BF16)


def per_device(cap, queries, kv_pool, block_table, lengths):
    nz = lax.axis_size("z")
    targets = nz * (cap + 1)

    def over_plane(x):
        turned = [
            ((y + NY // 2) % NY) * TP + (t + TP // 2) % TP for y in range(NY) for t in range(TP)
        ]
        return lax.all_to_all(
            x, ("y", "x", "c"), 0, 0, tiled=True, axis_index_groups=[turned]
        )

    def along_z(x):
        turned = [[(k + nz // 2) % nz for k in range(nz)]]
        x = lax.all_to_all(
            x.reshape(nz, -1, WIDE), "z", 0, 0, tiled=True, axis_index_groups=turned
        )
        return x.reshape(-1, WIDE)

    def pack(rows, skip):
        return call(
            functools.partial(pack_kernel, cap, skip),
            (shape(targets, WIDE), shape(MAXB * ROWS, targets)),
            [VMEM, HBM],
            [pltpu.VMEM((ROWS * 16, HD), F32)],
            (VMEM, VMEM),
        )(rows, kv_pool)

    def attend(got):
        return call(
            functools.partial(attend_kernel, cap),
            (shape(targets, WIDE), pltpu.SMEM((1,), jnp.int32)),
            [VMEM, VMEM],
            [
                pltpu.VMEM((SLOTS * GROUP, HD), F32),
                pltpu.VMEM((SLOTS * GROUP, HD), F32),
                pltpu.VMEM((SLOTS * GROUP, BLK), F32),
                pltpu.VMEM((SLOTS * GROUP, BLK), F32),
                pltpu.VMEM((SLOTS * GROUP, HD), F32),
            ],
            (VMEM, SMEM),
        )(got, kv_pool)

    def gather(places, backs):
        return call(
            functools.partial(gather_kernel, cap),
            shape(ROWS, 16, HD),
            [VMEM, VMEM],
            [pltpu.VMEM((ROWS * 16, HD), F32)],
        )(jnp.concatenate(places, axis=1), jnp.concatenate(backs, axis=0))

    def rounds(count):
        places, backs = [place], [back]
        for k in range(1, count):
            out, more = pack(rows, k * cap)
            places.append(more)
            backs.append(along_z(attend(along_z(out))[0]))
        return gather(places, backs)

    fanned = call(
        fan_kernel,
        shape(ROWS, 16, HD),
        [HBM, HBM, HBM],
        [
            pltpu.VMEM((1, TP * WIDE), BF16),
            pltpu.SMEM((MAXB, TP), jnp.int32),
            pltpu.SMEM((TP,), jnp.int32),
            pltpu.SemaphoreType.DMA((3,)),
        ],
    )(*(pltpu.with_memory_space_constraint(x, pltpu.HBM) for x in (queries, block_table.T, lengths)))
    rows = over_plane(fanned)
    out, place = pack(rows, 0)
    got = along_z(out)
    got, place, rows, kv_pool = lax.optimization_barrier((got, place, rows, kv_pool))
    back, over = attend(got)
    back = along_z(back)
    back, place, rows, over, kv_pool = lax.optimization_barrier((back, place, rows, over, kv_pool))
    mixed = gather([place], [back])
    mixed = lax.switch(
        over[0], [lambda: mixed, lambda: rounds(2), lambda: rounds(-(-SLOTS // cap))]
    )
    return call(finish_kernel, shape(1, TP * WIDE), [VMEM])(over_plane(mixed))


def solution(mesh):
    fine = Mesh(mesh.devices.reshape(-1, NY, TP // 2, 2), ("z", "y", "x", "c"))
    own = ("z", "y", "x", "c")
    return jax.shard_map(
        functools.partial(per_device, 7),
        mesh=fine,
        in_specs=(
            P(own, None),
            P(None, ("z", "y"), None, ("x", "c")),
            P(("z", "y"), None),
            P(("z", "y")),
        ),
        out_specs=P(own, None),
        check_vma=False,
    )
```

```python
import functools
import math

import jax
import jax.numpy as jnp
from jax import lax
from jax.experimental import pallas as pl
from jax.experimental.pallas import tpu as pltpu
from jax.sharding import Mesh, PartitionSpec as P

HD = 128
NY = 4
FAR = 4
TP = 8
GROUP = 8
MAXB = 4
BLK = 256
SLOTS = 32
ROWS = FAR * TP
WIDE = GROUP * HD
HALF = WIDE // 2
LONG = HALF + HD
SPAN = GROUP // 2
NEG = -1e30
F32 = jnp.float32
BF16 = jnp.bfloat16


def dot(a, b, dims):
    return lax.dot_general(a, b, (dims, ((), ())), preferred_element_type=F32)


def split(x):
    hi = x.astype(BF16).astype(F32)
    mid = (x - hi).astype(BF16).astype(F32)
    return hi, mid, x - hi - mid


def lanes(shape):
    return lax.broadcasted_iota(jnp.int32, shape, len(shape) - 1)


def up(shape):
    return lax.broadcasted_iota(jnp.int32, shape, 0)


def opposite(place, size):
    return jnp.where(place < size // 2, place + size // 2, place - size // 2)


def fan_kernel(q_hbm, table_hbm, len_hbm, out_ref, q_ref, table_ref, len_ref, sems):
    copies = [
        pltpu.make_async_copy(q_hbm, q_ref, sems.at[0]),
        pltpu.make_async_copy(table_hbm, table_ref, sems.at[1]),
        pltpu.make_async_copy(len_hbm, len_ref, sems.at[2]),
    ]
    for copy in copies:
        copy.start()
    for copy in copies:
        copy.wait()
    t = lax.axis_index("x") * 2 + lax.axis_index("c")
    lane = lanes((2 * TP, HD))
    extra = jnp.zeros((2 * TP, HD), F32)
    for b in range(MAXB):
        slot = table_ref[b, t]
        extra = jnp.where(lane == b, (slot // SLOTS).astype(F32), extra)
        extra = jnp.where(lane == MAXB + b, (slot % SLOTS).astype(F32), extra)
    length = len_ref[t]
    extra = jnp.where(lane == 8, (length // SLOTS).astype(F32), extra)
    extra = jnp.where(lane == 9, (length % SLOTS).astype(F32), extra)
    q = q_ref[...].astype(F32)
    halves = [q[:, i * HALF : (i + 1) * HALF] for i in range(2 * TP)]
    heads = jnp.concatenate(halves[TP:] + halves[:TP], axis=0)
    both = jnp.concatenate([heads, extra], axis=1).reshape(TP, 2, LONG).astype(BF16)
    for far in range(FAR):
        out_ref[far * TP : (far + 1) * TP] = both


def pack_kernel(cap, skip, a_ref, kv_hbm, out_ref, map_ref, scr):
    quarter = lax.axis_index("zh").astype(F32)
    targets = out_ref.shape[0]
    tall = cap + 1
    both = a_ref[...].astype(F32).reshape(ROWS * 2, LONG)
    for k in range(SPAN + 1):
        scr[k] = both[:, k * HD : (k + 1) * HD]
    query = jnp.concatenate(
        [scr[k, pl.ds(half, ROWS, stride=2), :] for half in range(2) for k in range(SPAN)], axis=1
    ).astype(BF16)
    extra = scr[SPAN, pl.ds(0, ROWS, stride=2), :].T
    pool = jnp.concatenate([extra[b : b + 1] for b in range(MAXB)], axis=1)
    slot = jnp.concatenate([extra[MAXB + b : MAXB + b + 1] for b in range(MAXB)], axis=1)
    length = extra[8:9] * SLOTS + extra[9:10]
    filled = jnp.concatenate([length - b * BLK for b in range(MAXB)], axis=1)
    filled = jnp.clip(filled, 0.0, float(BLK))
    planes = targets // tall
    holder = jnp.floor(pool * (1.0 / planes))
    dest = pool - holder * planes
    plane = jnp.floor(dest * (1.0 / NY))
    column = opposite(dest - plane * NY, NY)
    dest = opposite(plane, planes // NY) * NY + column
    valid = (holder == quarter) & (filled > 0.0)
    entries = MAXB * ROWS
    member = jnp.where((up((planes, entries)).astype(F32) == dest) & valid, 1.0, 0.0)
    earlier = jnp.where(up((entries, entries)) < lanes((entries, entries)), 1.0, 0.0)
    before = dot(member.astype(BF16), earlier.astype(BF16), ((1,), (0,)))
    rank = jnp.sum(before * member, axis=0, keepdims=True)
    most = jnp.max(jnp.sum(member, axis=1, keepdims=True), axis=0, keepdims=True)
    rank = rank - skip
    fits = valid & (rank >= 0.0) & (rank < cap)
    spot = up((targets, entries)).astype(F32)
    place = jnp.where(spot == jnp.where(fits, dest * tall + rank, -1.0), 1.0, 0.0)
    last = jnp.where(spot == jnp.where(fits, dest * tall + cap, -1.0), 1.0, 0.0).astype(BF16)
    side = up((HD, entries))
    mine = jnp.where(side % 2 == 0, slot + 1.0, filled)
    mine = jnp.where((side // 2).astype(F32) == rank, mine, 0.0).astype(BF16)
    four = jnp.concatenate([query] * MAXB, axis=0)
    out = dot(place.astype(BF16), four, ((1,), (0,)))
    out_ref[:, HD:] = out[:, HD:].astype(BF16)
    numbers = dot(last, mine, ((1,), (1,)))
    numbers = jnp.where(lanes((targets, HD)) == 2 * cap, most, numbers)
    final = up((targets, HD)) % tall == cap
    out_ref[:, :HD] = jnp.where(final, numbers, out[:, :HD]).astype(BF16)
    map_ref[...] = place.T.astype(BF16)


def own_lanes(x, tall, width):
    groups = x.shape[0] // tall
    x = x.astype(F32).reshape(groups, tall, HD)
    last = jnp.broadcast_to(x[:, tall - 1 : tall, :], (groups, tall, HD))
    row = lax.broadcasted_iota(jnp.int32, (groups, tall, HD), 1)
    mine = (lanes((groups, tall, HD)) // width == row) & (row < tall - 1)
    return jnp.where(mine, last, 0.0).reshape(groups * tall, HD)


def attend_kernel(cap, b_ref, kv_ref, out_ref, most_ref, q_scr, f_scr, s_scr, p_scr, o_scr):
    targets = b_ref.shape[0]
    tall = cap + 1
    numbers = b_ref[:, :HD]
    lane = lanes((targets, HD))
    row = lax.broadcasted_iota(jnp.int32, (targets, HD), 0)
    most = jnp.max(
        jnp.where((row % tall == cap) & (lane == 2 * cap), numbers.astype(F32), 0.0)
    )
    most_ref[0] = jnp.where(most > 2 * cap, 2, jnp.where(most > cap, 1, 0))
    own = own_lanes(numbers, tall, 2).astype(BF16)
    odd = jnp.where(lanes((8, HD)) % 2 == up((8, HD)), 1.0, 0.0).astype(BF16)
    pair = dot(odd, own, ((1,), (1,)))
    place = jnp.where(up((SLOTS, targets)).astype(F32) == pair[0:1] - 1.0, 1.0, 0.0)
    filled = jnp.sum(place * pair[1:2], axis=1, keepdims=True)
    filled = jnp.broadcast_to(filled, (SLOTS, HD))
    back_place = place.T.astype(BF16)
    got = dot(place.astype(BF16), b_ref[...], ((1,), (0,)))
    for g in range(GROUP):
        rows = pl.ds(g, SLOTS, stride=GROUP)
        q_scr[rows, :] = got[:, g * HD : (g + 1) * HD]
        f_scr[rows, :] = filled
    for s in range(SLOTS):
        rows = slice(s * GROUP, (s + 1) * GROUP)
        s_scr[rows, :] = dot(q_scr[rows, :].astype(BF16), kv_ref[0, s], ((1,), (1,)))
    scores = s_scr[...] * (1.0 / math.sqrt(HD))
    mask = lanes((SLOTS * GROUP, BLK)).astype(F32) < f_scr[:, 0:1]
    scores = jnp.where(mask, scores, NEG)
    peak = jnp.max(scores, axis=1, keepdims=True)
    expo = jnp.where(mask, jnp.exp(scores - peak), 0.0)
    total = jnp.sum(expo, axis=1, keepdims=True)
    used = total > 0.0
    total = jnp.where(used, total, 1.0)
    p_scr[...] = expo
    for s in range(SLOTS):
        rows = slice(s * GROUP, (s + 1) * GROUP)
        o_scr[rows, :] = dot(p_scr[rows, :].astype(BF16), kv_ref[1, s], ((1,), (0,)))
    o_scr[...] = o_scr[...] / total
    level = jnp.where(used, peak + jnp.log(total), NEG)
    f_scr[...] = jnp.broadcast_to(level, (SLOTS * GROUP, HD))
    lane = lanes((SLOTS, HD)) % 16
    coarse = jnp.zeros((SLOTS, HD), F32)
    fine = jnp.zeros((SLOTS, HD), F32)
    parts = []
    for g in range(GROUP):
        rows = pl.ds(g, SLOTS, stride=GROUP)
        parts.append(o_scr[rows, :])
        hi, mid, lo = split(f_scr[rows, :])
        coarse = jnp.where(lane == 2 * g, hi, jnp.where(lane == 2 * g + 1, mid, coarse))
        fine = jnp.where(lane == 2 * g, lo, fine)
    back = jnp.concatenate(parts, axis=1).astype(BF16)
    out = dot(back_place, back, ((1,), (0,)))
    out_ref[:, 2 * HD :] = out[:, 2 * HD :].astype(BF16)
    final = row % tall == cap
    lane = lanes((targets, HD))
    for k, part in enumerate((coarse, fine)):
        each = dot(back_place, part.astype(BF16), ((1,), (0,)))
        each = jnp.where(lane // 16 == row % tall, each, 0.0).reshape(targets // tall, tall, HD)
        both = jnp.broadcast_to(jnp.sum(each, axis=1, keepdims=True), each.shape)
        spot = slice(k * HD, (k + 1) * HD)
        out_ref[:, spot] = jnp.where(final, both.reshape(targets, HD), out[:, spot]).astype(BF16)


def gather_kernel(cap, map_ref, c_ref, out_ref, scr):
    tall = cap + 1
    coarse = own_lanes(c_ref[:, :HD], tall, 16).astype(BF16)
    fine = own_lanes(c_ref[:, HD : 2 * HD], tall, 16).astype(BF16)
    pick = up((HD, HD)) % 16 // 2 == lanes((HD, HD)) % GROUP
    pick = jnp.where(pick, 1.0, 0.0).astype(BF16)
    place = map_ref[...]
    got = dot(place, c_ref[...], ((1,), (0,)))
    level = 0.0
    for part in (coarse, fine):
        part = dot(place, part, ((1,), (0,))).astype(BF16)
        level = level + dot(part, pick, ((1,), (0,)))
    found = jnp.sum(place.astype(F32), axis=1, keepdims=True) > 0.0
    level = jnp.where(found, level, NEG)
    blocks = [slice(b * ROWS, (b + 1) * ROWS) for b in range(MAXB)]
    levels = [level[b] for b in blocks]
    ok = [found[b] for b in blocks]
    got = [got[b] for b in blocks]
    lane = lanes((ROWS, HD))
    top = functools.reduce(jnp.maximum, levels)
    factor = [jnp.where(o, jnp.exp(level - top), 0.0) for o, level in zip(ok, levels)]
    total = functools.reduce(jnp.add, factor)
    any_ok = total > 0.0
    total = jnp.where(any_ok, total, 1.0)
    three = split(jnp.where(any_ok, top + jnp.log(total), NEG))
    factor = [f / total for f in factor]
    extra = jnp.zeros((ROWS, HD), F32)
    for k, part in enumerate(three):
        extra = jnp.where(lane // GROUP == k, part, extra)
    for half in range(2):
        rows = pl.ds(half, ROWS, stride=2)
        for k in range(SPAN):
            g = half * SPAN + k
            mixed = [factor[b][:, g : g + 1] * got[b][:, g * HD : (g + 1) * HD] for b in range(MAXB)]
            scr[k, rows, :] = functools.reduce(jnp.add, mixed)
        scr[SPAN, rows, :] = extra
    both = jnp.concatenate([scr[k] for k in range(SPAN + 1)], axis=1)
    out_ref[...] = both.reshape(ROWS, 2, LONG).astype(BF16)


def finish_kernel(d_ref, out_ref):
    parts, level = [], []
    lane = lanes((2 * TP, HD))
    first = up((2 * TP, HD)) % 2 * SPAN
    mine = [(lane % GROUP == first + k) & (lane < 3 * GROUP) for k in range(SPAN)]
    for far in range(FAR):
        x = d_ref[far * TP : (far + 1) * TP].astype(F32).reshape(2 * TP, LONG)
        parts.append(x[:, :HALF])
        numbers = x[:, HALF:]
        level.append(
            [jnp.sum(jnp.where(m, numbers, 0.0), axis=1, keepdims=True) for m in mine]
        )
    result = []
    for k in range(SPAN):
        top = functools.reduce(jnp.maximum, [one[k] for one in level])
        factor = [jnp.exp(one[k] - top) for one in level]
        total = functools.reduce(jnp.add, factor)
        mixed = [f * p[:, k * HD : (k + 1) * HD] for f, p in zip(factor, parts)]
        result.append(functools.reduce(jnp.add, mixed) / total)
    result = jnp.concatenate(result, axis=1)
    halves = [result[i : i + 1] for i in range(2 * TP)]
    out_ref[...] = jnp.concatenate(halves[TP:] + halves[:TP], axis=1).astype(BF16)


SMEM = pl.BlockSpec(memory_space=pltpu.SMEM)
VMEM = pl.BlockSpec(memory_space=pltpu.VMEM)
HBM = pl.BlockSpec(memory_space=pltpu.HBM)


def call(kernel, out, ins, scratch=(), outs=VMEM, limit=24 << 20):
    return pl.pallas_call(
        kernel,
        out_shape=out,
        in_specs=ins,
        out_specs=outs,
        scratch_shapes=scratch,
        compiler_params=pltpu.CompilerParams(vmem_limit_bytes=limit),
    )


def shape(*dims):
    return jax.ShapeDtypeStruct(dims, BF16)


def per_device(cap, queries, kv_pool, block_table, lengths):
    near = ("zl", "y")
    pools = lax.axis_size(near)
    targets = pools * (cap + 1)

    def turned(slow, fast):
        return [[(i + slow // 2) % slow * fast + (j + fast // 2) % fast for i in range(slow) for j in range(fast)]]

    def over_far(x):
        return lax.all_to_all(
            x, ("zh", "x", "c"), 0, 0, tiled=True, axis_index_groups=turned(FAR, TP)
        )

    def over_near(x):
        x = x.reshape(pools, -1, WIDE)
        groups = turned(pools // NY, NY)
        x = lax.all_to_all(x, near, 0, 0, tiled=True, axis_index_groups=groups)
        return x.reshape(-1, WIDE)

    def pack(rows, skip):
        return call(
            functools.partial(pack_kernel, cap, skip),
            (shape(targets, WIDE), shape(MAXB * ROWS, targets)),
            [VMEM, HBM],
            [pltpu.VMEM((SPAN + 1, ROWS * 2, HD), F32)],
            (VMEM, VMEM),
        )(rows, kv_pool)

    def attend(got):
        return call(
            functools.partial(attend_kernel, cap),
            (shape(targets, WIDE), pltpu.SMEM((1,), jnp.int32)),
            [VMEM, VMEM],
            [
                pltpu.VMEM((SLOTS * GROUP, HD), F32),
                pltpu.VMEM((SLOTS * GROUP, HD), F32),
                pltpu.VMEM((SLOTS * GROUP, BLK), F32),
                pltpu.VMEM((SLOTS * GROUP, BLK), F32),
                pltpu.VMEM((SLOTS * GROUP, HD), F32),
            ],
            (VMEM, SMEM),
        )(got, kv_pool)

    def gather(places, backs):
        return call(
            functools.partial(gather_kernel, cap),
            shape(ROWS, 2, LONG),
            [VMEM, VMEM],
            [pltpu.VMEM((SPAN + 1, ROWS * 2, HD), F32)],
        )(jnp.concatenate(places, axis=1), jnp.concatenate(backs, axis=0))

    def rounds(count):
        places, backs = [place], [back]
        for k in range(1, count):
            out, more = pack(rows, k * cap)
            places.append(more)
            backs.append(over_near(attend(over_near(out))[0]))
        return gather(places, backs)

    fanned = call(
        fan_kernel,
        shape(ROWS, 2, LONG),
        [HBM, HBM, HBM],
        [
            pltpu.VMEM((1, TP * WIDE), BF16),
            pltpu.SMEM((MAXB, TP), jnp.int32),
            pltpu.SMEM((TP,), jnp.int32),
            pltpu.SemaphoreType.DMA((3,)),
        ],
    )(*(pltpu.with_memory_space_constraint(x, pltpu.HBM) for x in (queries, block_table.T, lengths)))
    rows = over_far(fanned)
    out, place = pack(rows, 0)
    got = over_near(out)
    got, place, rows, kv_pool = lax.optimization_barrier((got, place, rows, kv_pool))
    back, over = attend(got)
    back = over_near(back)
    back, place, rows, over, kv_pool = lax.optimization_barrier((back, place, rows, over, kv_pool))
    mixed = gather([place], [back])
    mixed = lax.switch(
        over[0], [lambda: mixed, lambda: rounds(2), lambda: rounds(-(-SLOTS // cap))]
    )
    return call(finish_kernel, shape(1, TP * WIDE), [VMEM])(over_far(mixed))


def solution(mesh):
    fine = Mesh(
        mesh.devices.reshape(FAR, -1, NY, TP // 2, 2), ("zh", "zl", "y", "x", "c")
    )
    own = fine.axis_names
    return jax.shard_map(
        functools.partial(per_device, 7),
        mesh=fine,
        in_specs=(
            P(own, None),
            P(None, own[:3], None, own[3:]),
            P(own[:3], None),
            P(own[:3]),
        ),
        out_specs=P(own, None),
        check_vma=False,
    )
```

```python
import functools
import math

import jax
import jax.numpy as jnp
from jax import lax
from jax.experimental import pallas as pl
from jax.experimental.pallas import tpu as pltpu
from jax.sharding import Mesh, PartitionSpec as P

HD = 128
NY = 4
FAR = 4
TP = 8
GROUP = 8
MAXB = 4
BLK = 256
SLOTS = 32
ROWS = FAR * TP
WIDE = GROUP * HD
HALF = WIDE // 2
LONG = HALF + HD
SPAN = GROUP // 2
NEG = -1e30
F32 = jnp.float32
BF16 = jnp.bfloat16


def dot(a, b, dims):
    return lax.dot_general(a, b, (dims, ((), ())), preferred_element_type=F32)


def split(x):
    hi = x.astype(BF16).astype(F32)
    mid = (x - hi).astype(BF16).astype(F32)
    return hi, mid, x - hi - mid


def lanes(shape):
    return lax.broadcasted_iota(jnp.int32, shape, len(shape) - 1)


def up(shape):
    return lax.broadcasted_iota(jnp.int32, shape, 0)


def opposite(place, size):
    return jnp.where(place < size // 2, place + size // 2, place - size // 2)


def fan_kernel(q_hbm, table_hbm, len_hbm, out_ref, q_ref, table_ref, len_ref, sems):
    copies = [
        pltpu.make_async_copy(q_hbm, q_ref, sems.at[0]),
        pltpu.make_async_copy(table_hbm, table_ref, sems.at[1]),
        pltpu.make_async_copy(len_hbm, len_ref, sems.at[2]),
    ]
    for copy in copies:
        copy.start()
    for copy in copies:
        copy.wait()
    t = lax.axis_index("x") * 2 + lax.axis_index("c")
    lane = lanes((2 * TP, HD))
    extra = jnp.zeros((2 * TP, HD), F32)
    for b in range(MAXB):
        slot = table_ref[b, t]
        extra = jnp.where(lane == b, (slot // SLOTS).astype(F32), extra)
        extra = jnp.where(lane == MAXB + b, (slot % SLOTS).astype(F32), extra)
    length = len_ref[t]
    extra = jnp.where(lane == 8, (length // SLOTS).astype(F32), extra)
    extra = jnp.where(lane == 9, (length % SLOTS).astype(F32), extra)
    q = q_ref[...].astype(F32)
    halves = [q[:, i * HALF : (i + 1) * HALF] for i in range(2 * TP)]
    order = [(p + TP // 2) % TP ^ 1 for p in range(TP)]
    heads = jnp.concatenate([halves[2 * p + half] for p in order for half in range(2)], axis=0)
    both = jnp.concatenate([heads, extra], axis=1).reshape(TP, 2, LONG).astype(BF16)
    for far in range(FAR):
        out_ref[far * TP : (far + 1) * TP] = both


def pack_kernel(cap, skip, a_ref, kv_hbm, out_ref, map_ref, scr):
    quarter = lax.axis_index("zh").astype(F32)
    targets = out_ref.shape[0]
    tall = cap + 1
    both = a_ref[...].astype(F32).reshape(ROWS * 2, LONG)
    for k in range(SPAN + 1):
        scr[k] = both[:, k * HD : (k + 1) * HD]
    def take(k, half):
        parts = [scr[k, pl.ds(2 * c + half, ROWS // 2, stride=4), :] for c in range(2)]
        return jnp.concatenate(parts, axis=0)

    query = jnp.concatenate(
        [take(k, half) for half in range(2) for k in range(SPAN)], axis=1
    ).astype(BF16)
    extra = take(SPAN, 0).T
    pool = jnp.concatenate([extra[b : b + 1] for b in range(MAXB)], axis=1)
    slot = jnp.concatenate([extra[MAXB + b : MAXB + b + 1] for b in range(MAXB)], axis=1)
    length = extra[8:9] * SLOTS + extra[9:10]
    filled = jnp.concatenate([length - b * BLK for b in range(MAXB)], axis=1)
    filled = jnp.clip(filled, 0.0, float(BLK))
    planes = targets // tall
    holder = jnp.floor(pool * (1.0 / planes))
    dest = pool - holder * planes
    plane = jnp.floor(dest * (1.0 / NY))
    column = opposite(dest - plane * NY, NY)
    dest = opposite(plane, planes // NY) * NY + column
    valid = (holder == quarter) & (filled > 0.0)
    entries = MAXB * ROWS
    member = jnp.where((up((planes, entries)).astype(F32) == dest) & valid, 1.0, 0.0)
    earlier = jnp.where(up((entries, entries)) < lanes((entries, entries)), 1.0, 0.0)
    before = dot(member.astype(BF16), earlier.astype(BF16), ((1,), (0,)))
    rank = jnp.sum(before * member, axis=0, keepdims=True)
    most = jnp.max(jnp.sum(member, axis=1, keepdims=True), axis=0, keepdims=True)
    rank = rank - skip
    fits = valid & (rank >= 0.0) & (rank < cap)
    spot = up((targets, entries)).astype(F32)
    place = jnp.where(spot == jnp.where(fits, dest * tall + rank, -1.0), 1.0, 0.0)
    last = jnp.where(spot == jnp.where(fits, dest * tall + cap, -1.0), 1.0, 0.0).astype(BF16)
    side = up((HD, entries))
    mine = jnp.where(side % 2 == 0, slot + 1.0, filled)
    mine = jnp.where((side // 2).astype(F32) == rank, mine, 0.0).astype(BF16)
    four = jnp.concatenate([query] * MAXB, axis=0)
    out = dot(place.astype(BF16), four, ((1,), (0,)))
    out_ref[:, HD:] = out[:, HD:].astype(BF16)
    numbers = dot(last, mine, ((1,), (1,)))
    numbers = jnp.where(lanes((targets, HD)) == 2 * cap, most, numbers)
    final = up((targets, HD)) % tall == cap
    out_ref[:, :HD] = jnp.where(final, numbers, out[:, :HD]).astype(BF16)
    map_ref[...] = place.T.astype(BF16)


def own_lanes(x, tall, width):
    groups = x.shape[0] // tall
    x = x.astype(F32).reshape(groups, tall, HD)
    last = jnp.broadcast_to(x[:, tall - 1 : tall, :], (groups, tall, HD))
    row = lax.broadcasted_iota(jnp.int32, (groups, tall, HD), 1)
    mine = (lanes((groups, tall, HD)) // width == row) & (row < tall - 1)
    return jnp.where(mine, last, 0.0).reshape(groups * tall, HD)


def attend_kernel(cap, b_ref, kv_ref, out_ref, most_ref, q_scr, f_scr, s_scr, p_scr, o_scr):
    targets = b_ref.shape[0]
    tall = cap + 1
    numbers = b_ref[:, :HD]
    lane = lanes((targets, HD))
    row = lax.broadcasted_iota(jnp.int32, (targets, HD), 0)
    most = jnp.max(
        jnp.where((row % tall == cap) & (lane == 2 * cap), numbers.astype(F32), 0.0)
    )
    most_ref[0] = jnp.where(most > 2 * cap, 2, jnp.where(most > cap, 1, 0))
    own = own_lanes(numbers, tall, 2).astype(BF16)
    odd = jnp.where(lanes((8, HD)) % 2 == up((8, HD)), 1.0, 0.0).astype(BF16)
    pair = dot(odd, own, ((1,), (1,)))
    place = jnp.where(up((SLOTS, targets)).astype(F32) == pair[0:1] - 1.0, 1.0, 0.0)
    filled = jnp.sum(place * pair[1:2], axis=1, keepdims=True)
    filled = jnp.broadcast_to(filled, (SLOTS, HD))
    back_place = place.T.astype(BF16)
    got = dot(place.astype(BF16), b_ref[...], ((1,), (0,)))
    for g in range(GROUP):
        rows = pl.ds(g, SLOTS, stride=GROUP)
        q_scr[rows, :] = got[:, g * HD : (g + 1) * HD]
        f_scr[rows, :] = filled
    for s in range(SLOTS):
        rows = slice(s * GROUP, (s + 1) * GROUP)
        s_scr[rows, :] = dot(q_scr[rows, :].astype(BF16), kv_ref[0, s], ((1,), (1,)))
    scores = s_scr[...] * (1.0 / math.sqrt(HD))
    mask = lanes((SLOTS * GROUP, BLK)).astype(F32) < f_scr[:, 0:1]
    scores = jnp.where(mask, scores, NEG)
    peak = jnp.max(scores, axis=1, keepdims=True)
    expo = jnp.where(mask, jnp.exp(scores - peak), 0.0)
    total = jnp.sum(expo, axis=1, keepdims=True)
    used = total > 0.0
    total = jnp.where(used, total, 1.0)
    p_scr[...] = expo
    for s in range(SLOTS):
        rows = slice(s * GROUP, (s + 1) * GROUP)
        o_scr[rows, :] = dot(p_scr[rows, :].astype(BF16), kv_ref[1, s], ((1,), (0,)))
    o_scr[...] = o_scr[...] / total
    level = jnp.where(used, peak + jnp.log(total), NEG)
    f_scr[...] = jnp.broadcast_to(level, (SLOTS * GROUP, HD))
    lane = lanes((SLOTS, HD)) % 16
    coarse = jnp.zeros((SLOTS, HD), F32)
    fine = jnp.zeros((SLOTS, HD), F32)
    parts = []
    for g in range(GROUP):
        rows = pl.ds(g, SLOTS, stride=GROUP)
        parts.append(o_scr[rows, :])
        hi, mid, lo = split(f_scr[rows, :])
        coarse = jnp.where(lane == 2 * g, hi, jnp.where(lane == 2 * g + 1, mid, coarse))
        fine = jnp.where(lane == 2 * g, lo, fine)
    back = jnp.concatenate(parts, axis=1).astype(BF16)
    out = dot(back_place, back, ((1,), (0,)))
    out_ref[:, 2 * HD :] = out[:, 2 * HD :].astype(BF16)
    final = row % tall == cap
    lane = lanes((targets, HD))
    for k, part in enumerate((coarse, fine)):
        each = dot(back_place, part.astype(BF16), ((1,), (0,)))
        each = jnp.where(lane // 16 == row % tall, each, 0.0).reshape(targets // tall, tall, HD)
        both = jnp.broadcast_to(jnp.sum(each, axis=1, keepdims=True), each.shape)
        spot = slice(k * HD, (k + 1) * HD)
        out_ref[:, spot] = jnp.where(final, both.reshape(targets, HD), out[:, spot]).astype(BF16)


def gather_kernel(cap, map_ref, c_ref, out_ref, scr):
    tall = cap + 1
    coarse = own_lanes(c_ref[:, :HD], tall, 16).astype(BF16)
    fine = own_lanes(c_ref[:, HD : 2 * HD], tall, 16).astype(BF16)
    pick = up((HD, HD)) % 16 // 2 == lanes((HD, HD)) % GROUP
    pick = jnp.where(pick, 1.0, 0.0).astype(BF16)
    place = map_ref[...]
    got = dot(place, c_ref[...], ((1,), (0,)))
    level = 0.0
    for part in (coarse, fine):
        part = dot(place, part, ((1,), (0,))).astype(BF16)
        level = level + dot(part, pick, ((1,), (0,)))
    found = jnp.sum(place.astype(F32), axis=1, keepdims=True) > 0.0
    level = jnp.where(found, level, NEG)
    blocks = [slice(b * ROWS, (b + 1) * ROWS) for b in range(MAXB)]
    levels = [level[b] for b in blocks]
    ok = [found[b] for b in blocks]
    got = [got[b] for b in blocks]
    lane = lanes((ROWS, HD))
    top = functools.reduce(jnp.maximum, levels)
    factor = [jnp.where(o, jnp.exp(level - top), 0.0) for o, level in zip(ok, levels)]
    total = functools.reduce(jnp.add, factor)
    any_ok = total > 0.0
    total = jnp.where(any_ok, total, 1.0)
    three = split(jnp.where(any_ok, top + jnp.log(total), NEG))
    factor = [f / total for f in factor]
    extra = jnp.zeros((ROWS, HD), F32)
    for k, part in enumerate(three):
        extra = jnp.where(lane // GROUP == k, part, extra)

    def put(k, half, x):
        for c in range(2):
            rows = pl.ds(2 * (1 - c) + half, ROWS // 2, stride=4)
            scr[k, rows, :] = x[c * ROWS // 2 : (c + 1) * ROWS // 2]

    for half in range(2):
        for k in range(SPAN):
            g = half * SPAN + k
            mixed = [factor[b][:, g : g + 1] * got[b][:, g * HD : (g + 1) * HD] for b in range(MAXB)]
            put(k, half, functools.reduce(jnp.add, mixed))
        put(SPAN, half, extra)
    both = jnp.concatenate([scr[k] for k in range(SPAN + 1)], axis=1)
    out_ref[...] = both.reshape(ROWS, 2, LONG).astype(BF16)


def finish_kernel(d_ref, out_ref):
    parts, level = [], []
    lane = lanes((2 * TP, HD))
    first = up((2 * TP, HD)) % 2 * SPAN
    mine = [(lane % GROUP == first + k) & (lane < 3 * GROUP) for k in range(SPAN)]
    for far in range(FAR):
        x = d_ref[far * TP : (far + 1) * TP].astype(F32).reshape(2 * TP, LONG)
        parts.append(x[:, :HALF])
        numbers = x[:, HALF:]
        level.append(
            [jnp.sum(jnp.where(m, numbers, 0.0), axis=1, keepdims=True) for m in mine]
        )
    result = []
    for k in range(SPAN):
        top = functools.reduce(jnp.maximum, [one[k] for one in level])
        factor = [jnp.exp(one[k] - top) for one in level]
        total = functools.reduce(jnp.add, factor)
        mixed = [f * p[:, k * HD : (k + 1) * HD] for f, p in zip(factor, parts)]
        result.append(functools.reduce(jnp.add, mixed) / total)
    result = jnp.concatenate(result, axis=1)
    halves = [result[i : i + 1] for i in range(2 * TP)]
    out_ref[...] = jnp.concatenate(halves[TP:] + halves[:TP], axis=1).astype(BF16)


SMEM = pl.BlockSpec(memory_space=pltpu.SMEM)
VMEM = pl.BlockSpec(memory_space=pltpu.VMEM)
HBM = pl.BlockSpec(memory_space=pltpu.HBM)


def call(kernel, out, ins, scratch=(), outs=VMEM, limit=24 << 20):
    return pl.pallas_call(
        kernel,
        out_shape=out,
        in_specs=ins,
        out_specs=outs,
        scratch_shapes=scratch,
        compiler_params=pltpu.CompilerParams(vmem_limit_bytes=limit),
    )


def shape(*dims):
    return jax.ShapeDtypeStruct(dims, BF16)


def per_device(cap, queries, kv_pool, block_table, lengths):
    near = ("zl", "y")
    pools = lax.axis_size(near)
    targets = pools * (cap + 1)

    def turned(slow, fast):
        return [[(i + slow // 2) % slow * fast + (j + fast // 2) % fast for i in range(slow) for j in range(fast)]]

    def over_far(x, core):
        groups = [[place ^ core for place in turned(FAR, TP)[0]]]
        return lax.all_to_all(
            x, ("zh", "x", "c"), 0, 0, tiled=True, axis_index_groups=groups
        )

    def over_near(x):
        x = x.reshape(pools, -1, WIDE)
        groups = turned(pools // NY, NY)
        x = lax.all_to_all(x, near, 0, 0, tiled=True, axis_index_groups=groups)
        return x.reshape(-1, WIDE)

    def pack(rows, skip):
        return call(
            functools.partial(pack_kernel, cap, skip),
            (shape(targets, WIDE), shape(MAXB * ROWS, targets)),
            [VMEM, HBM],
            [pltpu.VMEM((SPAN + 1, ROWS * 2, HD), F32)],
            (VMEM, VMEM),
        )(rows, kv_pool)

    def attend(got):
        return call(
            functools.partial(attend_kernel, cap),
            (shape(targets, WIDE), pltpu.SMEM((1,), jnp.int32)),
            [VMEM, VMEM],
            [
                pltpu.VMEM((SLOTS * GROUP, HD), F32),
                pltpu.VMEM((SLOTS * GROUP, HD), F32),
                pltpu.VMEM((SLOTS * GROUP, BLK), F32),
                pltpu.VMEM((SLOTS * GROUP, BLK), F32),
                pltpu.VMEM((SLOTS * GROUP, HD), F32),
            ],
            (VMEM, SMEM),
        )(got, kv_pool)

    def gather(places, backs):
        return call(
            functools.partial(gather_kernel, cap),
            shape(ROWS, 2, LONG),
            [VMEM, VMEM],
            [pltpu.VMEM((SPAN + 1, ROWS * 2, HD), F32)],
        )(jnp.concatenate(places, axis=1), jnp.concatenate(backs, axis=0))

    def rounds(count):
        places, backs = [place], [back]
        for k in range(1, count):
            out, more = pack(rows, k * cap)
            places.append(more)
            backs.append(over_near(attend(over_near(out))[0]))
        return gather(places, backs)

    fanned = call(
        fan_kernel,
        shape(ROWS, 2, LONG),
        [HBM, HBM, HBM],
        [
            pltpu.VMEM((1, TP * WIDE), BF16),
            pltpu.SMEM((MAXB, TP), jnp.int32),
            pltpu.SMEM((TP,), jnp.int32),
            pltpu.SemaphoreType.DMA((3,)),
        ],
    )(*(pltpu.with_memory_space_constraint(x, pltpu.HBM) for x in (queries, block_table.T, lengths)))
    rows = over_far(fanned, 1)
    out, place = pack(rows, 0)
    got = over_near(out)
    got, place, rows, kv_pool = lax.optimization_barrier((got, place, rows, kv_pool))
    back, over = attend(got)
    back = over_near(back)
    back, place, rows, over, kv_pool = lax.optimization_barrier((back, place, rows, over, kv_pool))
    mixed = gather([place], [back])
    mixed = lax.switch(
        over[0], [lambda: mixed, lambda: rounds(2), lambda: rounds(-(-SLOTS // cap))]
    )
    return call(finish_kernel, shape(1, TP * WIDE), [VMEM])(over_far(mixed, 0))


def solution(mesh):
    fine = Mesh(
        mesh.devices.reshape(FAR, -1, NY, TP // 2, 2), ("zh", "zl", "y", "x", "c")
    )
    own = fine.axis_names
    return jax.shard_map(
        functools.partial(per_device, 7),
        mesh=fine,
        in_specs=(
            P(own, None),
            P(None, own[:3], None, own[3:]),
            P(own[:3], None),
            P(own[:3]),
        ),
        out_specs=P(own, None),
        check_vma=False,
    )
```
